32 devices in a mesh: ctx: 16 (over z, x, core), head: 2 (over y).
Axes of the slice: x: 2, y: 2, z: 4, core: 2. Of those that a mesh axis runs over, the one named last changes fastest.
Arguments:
- queries: bfloat16 [4096, 4096], P(('ctx', 'head')), may hold values from -6 to 6
- key_rows: bfloat16 [4096, 4096], P(('ctx', 'head')), may hold values from -6 to 6
- value_rows: bfloat16 [4096, 4096], P(('ctx', 'head')), may hold values from -6 to 6
- grad_out: bfloat16 [4096, 4096], P(('ctx', 'head')), may hold values from -6 to 6
Outputs:
- grad_query: bfloat16 [4096, 4096], P(('ctx', 'head'))
- grad_key: bfloat16 [4096, 4096], P(('ctx', 'head'))
- grad_value: bfloat16 [4096, 4096], P(('ctx', 'head'))
The draws below stay inside these ranges and needn't reach their ends.
All inputs are finite; a program needn't handle non-finite values.
Results may differ from the reference program's by a relative error of at most 0.0021.
Values may be sent and summed in bfloat16 or wider, within the bound.
No kernel may reach another device: no remote copies, remote signals or barrier semaphores. Data moves between devices by JAX's collectives and lax.ppermute only.
A program may use at most 128 MiB of HBM per device.

```python
import jax
import jax.numpy as jnp
from jax import lax

HEADS = 32
HEAD_DIM = 128
SEQ = 4096
GROUP = 128


def block_scale(stream_key, extent, cuts, smallest, high):
    def one(dim, blocks):
        steps = jax.random.uniform(jax.random.fold_in(jax.random.fold_in(stream_key, 6), dim), (blocks,), jnp.float32, smallest / len(cuts), high / len(cuts))
        return jnp.repeat(jnp.exp(steps), extent[dim] // blocks).reshape((-1,) + (1,) * (len(extent) - dim - 1))

    gain = one(*cuts[0])
    for cut in cuts[1:]:
        gain = gain * one(*cut)
    return gain


def normal_values(key, shape, scale, most, cuts=(), held_as=jnp.bfloat16):
    gain = block_scale(key, shape, cuts, -0.22, 0.18) if cuts else 1.0
    drawn = jax.random.normal(key, shape, jnp.float32) * scale * gain
    return jnp.minimum(jnp.maximum(drawn, -most), most).astype(held_as)


def setup_inputs(seed: int = 0) -> dict:
    key_of = jax.random.split(jax.random.key(seed), 5)
    return {
        "queries": normal_values(key_of[0], (SEQ, HEADS * HEAD_DIM), 1.0, 6.0, ((0, 32),)),
        "key_rows": normal_values(key_of[1], (SEQ, HEADS * HEAD_DIM), 1.0, 6.0, ((0, 32),)),
        "value_rows": normal_values(key_of[2], (SEQ, HEADS * HEAD_DIM), 1.0, 6.0, ((0, 32),)),
        "grad_out": normal_values(key_of[3], (SEQ, HEADS * HEAD_DIM), 1.0, 6.0, ((0, 32),)),
    }


def reference(queries, key_rows, value_rows, grad_out):
    blk = GROUP
    count = SEQ // blk
    scale = (HEAD_DIM * SEQ) ** -0.5
    highest = lax.Precision.HIGHEST
    mask = jnp.tril(jnp.ones((blk, blk), jnp.float32))

    def split(array):
        return array.reshape(count, blk, HEADS, HEAD_DIM)

    blocks = (split(queries), split(key_rows), split(value_rows), split(grad_out))

    def prepare(pieces):
        qf, kf, vf, df = [piece.astype(jnp.float32) for piece in pieces]
        scores = (jnp.einsum("thd,shd->hts", qf, kf, precision=highest) * (scale * mask)).astype(jnp.bfloat16)
        dscores = (jnp.einsum("thd,shd->hts", df, vf, precision=highest) * mask).astype(jnp.bfloat16)
        return qf, kf, vf, df, scores.astype(jnp.float32), dscores.astype(jnp.float32)

    def forward_step(kv_state, pieces):
        qf, kf, vf, df, scores, dscores = prepare(pieces)
        grad_q = scale * (jnp.einsum("hts,shd->thd", dscores, kf, precision=highest)
                          + jnp.einsum("tha,hab->thb", df, kv_state, precision=highest))
        kv_state = kv_state + jnp.einsum("tha,thb->hab", vf, kf, precision=highest)
        return kv_state, grad_q.astype(jnp.bfloat16)

    def backward_step(grad_state, pieces):
        qf, kf, vf, df, scores, dscores = prepare(pieces)
        grad_k = scale * (jnp.einsum("hts,thd->shd", dscores, qf, precision=highest)
                          + jnp.einsum("tha,hab->thb", vf, grad_state, precision=highest))
        grad_v = (jnp.einsum("hts,thd->shd", scores, df, precision=highest)
                  + scale * jnp.einsum("thb,hab->tha", kf, grad_state, precision=highest))
        grad_state = grad_state + jnp.einsum("tha,thb->hab", df, qf, precision=highest)
        return grad_state, (grad_k.astype(jnp.bfloat16), grad_v.astype(jnp.bfloat16))

    start = jnp.zeros((HEADS, HEAD_DIM, HEAD_DIM), jnp.float32)
    unused, grad_q = lax.scan(forward_step, start, blocks)
    unused_too, (grad_k, grad_v) = lax.scan(backward_step, start, blocks, reverse=True)
    width = HEADS * HEAD_DIM
    return (grad_q.reshape(SEQ, width), grad_k.reshape(SEQ, width), grad_v.reshape(SEQ, width))
```

```python
import functools

import jax
import jax.numpy as jnp
from jax import lax
from jax.experimental import pallas as pl
from jax.experimental.pallas import tpu as pltpu
from jax.sharding import PartitionSpec as P

HEAD_DIM = 128
GROUP = 128
AXES = ("ctx", "head")
F32 = jnp.float32
BF16 = jnp.bfloat16
HALF = jnp.float16
TAIL = 16
TOP = 15.0


def dot(a, b, dims):
    return lax.dot_general(a, b, (dims, ((), ())), preferred_element_type=F32)


def state_kernel(order, q0, k0, v0, d0, q1, k1, v1, d1, mine, sent, most):
    step = pl.program_id(0)

    @pl.when(step == 0)
    def _():
        most[...] = jnp.zeros_like(most)

    for refs, out in (((q0, k0, v0, d0), mine), ((q1, k1, v1, d1), sent)):
        q, k, v, d = refs
        for head in range(q.shape[1] // HEAD_DIM):
            cols = slice(head * HEAD_DIM, (head + 1) * HEAD_DIM)
            for kind, (left, right) in enumerate(((v, k), (d, q))):
                state = dot(left[:, cols], right[:, cols], ((0,), (0,)))
                out[0, kind, cols, :] = state
                peak = jnp.max(jnp.abs(state).reshape(HEAD_DIM // 8, 8, HEAD_DIM), axis=0)
                rows = slice(kind * 8, kind * 8 + 8)
                most[rows, :] = jnp.maximum(most[rows, :], peak)

    @pl.when(step == pl.num_programs(0) - 1)
    def _():
        for kind in range(2):
            rows = slice(kind * 8, kind * 8 + 8)
            most[rows, :] = jnp.full((8, HEAD_DIM), jnp.max(most[rows, :]), F32)


def states(order, arrays, width):
    rows = arrays[0].shape[0]
    specs = [pl.BlockSpec((rows, width), lambda i, o: (0, o[i]))] * 4
    specs += [pl.BlockSpec((rows, width), lambda i, o: (0, o[i + 4]))] * 4
    block = pl.BlockSpec((1, 2, width, HEAD_DIM), lambda i, o: (i, 0, 0, 0))
    shape = jax.ShapeDtypeStruct((4, 2, width, HEAD_DIM), F32)
    return pl.pallas_call(
        state_kernel,
        grid_spec=pltpu.PrefetchScalarGridSpec(
            num_scalar_prefetch=1,
            grid=(4,),
            in_specs=specs,
            out_specs=(block, block, pl.BlockSpec((16, HEAD_DIM), lambda i, o: (0, 0))),
        ),
        out_shape=(shape, shape, jax.ShapeDtypeStruct((16, HEAD_DIM), F32)),
        cost_estimate=pl.CostEstimate(
            flops=32 * rows * width * HEAD_DIM, bytes_accessed=24 * rows * width * 8, transcendentals=0
        ),
        name="group_states",
    )(order, *arrays, *arrays)


def gradient_kernel(scale, order, q, k, v, d, state, *rest):
    gq, gk, gv = rest[-3:]
    rows = q.shape[0]
    later = lax.broadcasted_iota(jnp.int32, (rows, rows), 0)
    earlier = lax.broadcasted_iota(jnp.int32, (rows, rows), 1)
    causal = later >= earlier
    nn, nt, tn = ((1,), (0,)), ((1,), (1,)), ((0,), (0,))
    for head in range(q.shape[1] // HEAD_DIM):
        cols = slice(head * HEAD_DIM, (head + 1) * HEAD_DIM)
        qh, kh, vh, dh = q[:, cols], k[:, cols], v[:, cols], d[:, cols]
        scores = jnp.where(causal, dot(qh, kh, nt) * scale, 0.0).astype(BF16)
        dscores = jnp.where(causal, dot(dh, vh, nt), 0.0).astype(BF16)
        kv, g = state[0, 0, cols, :], state[0, 1, cols, :]
        kv_hi, g_hi = kv.astype(BF16), g.astype(BF16)
        kv_lo = (kv - kv_hi.astype(F32)).astype(BF16)
        g_lo = (g - g_hi.astype(F32)).astype(BF16)
        out_q = dot(dscores, kh, nn) + (dot(dh, kv_hi, nn) + dot(dh, kv_lo, nn))
        out_k = dot(dscores, qh, tn) + (dot(vh, g_hi, nn) + dot(vh, g_lo, nn))
        out_v = dot(scores, dh, tn) + scale * (dot(kh, g_hi, nt) + dot(kh, g_lo, nt))
        gq[:, cols] = (out_q * scale).astype(BF16)
        gk[:, cols] = (out_k * scale).astype(BF16)
        gv[:, cols] = out_v.astype(BF16)


def gradients(order, arrays, state, scale, width, before):
    rows, columns = arrays[0].shape
    block = pl.BlockSpec((rows, width), lambda i, o: (0, o[i]))
    shape = jax.ShapeDtypeStruct((rows, columns), BF16)
    extra = () if before is None else tuple(before)
    return pl.pallas_call(
        functools.partial(gradient_kernel, scale),
        grid_spec=pltpu.PrefetchScalarGridSpec(
            num_scalar_prefetch=1,
            grid=(4,),
            in_specs=[block] * 4
            + [pl.BlockSpec((1, 2, width, HEAD_DIM), lambda i, o: (i, 0, 0, 0))]
            + [pl.BlockSpec(memory_space=pl.ANY)] * len(extra),
            out_specs=(block,) * 3,
        ),
        out_shape=(shape,) * 3,
        input_output_aliases={6 + i: i for i in range(len(extra))},
        cost_estimate=pl.CostEstimate(
            flops=88 * rows * width * HEAD_DIM, bytes_accessed=88 * rows * width, transcendentals=0
        ),
        name="group_gradients",
    )(order, *arrays, state, *extra)


def exponents(bound):
    return jnp.clip(jnp.ceil(jnp.log2(jnp.maximum(bound, 1e-30))) + 1.0, -100.0, 60.0)


def per_kind(rows):
    return rows.reshape(2, 8, HEAD_DIM)[:, :1, :]


def encode(parts, exps):
    factor = jnp.exp2(TOP - exps)
    factor = per_kind(factor)
    flat = [(part * factor[: part.shape[0]]).reshape(-1, HEAD_DIM) for part in parts]
    return jnp.concatenate(flat + [exps], axis=0).astype(HALF)


def exponents_of(message):
    return message[-TAIL:].astype(F32)


def decode(rows, exps, kinds):
    factor = per_kind(jnp.exp2(exps - TOP))
    return rows.reshape(kinds, -1, HEAD_DIM).astype(F32) * factor[:kinds]


def whole_groups(queries, key_rows, value_rows, grad_out):
    arrays = (queries, key_rows, value_rows, grad_out)
    rows = queries.shape[0]
    heads = queries.shape[1] // HEAD_DIM
    n_ctx, n_head = lax.axis_size("ctx"), lax.axis_size("head")
    devices = n_ctx * n_head
    place = lax.axis_index("ctx") * n_head + lax.axis_index("head")
    scale = (HEAD_DIM * rows * devices) ** (-0.5)
    outer = (devices // 8).bit_length() - 1
    per = heads // 8

    def move(x, mask):
        return lax.ppermute(x, AXES, [(p, p ^ mask) for p in range(devices)])

    bit = [((place >> b) & 1).astype(F32) for b in range(3 + outer)]

    def weight(b):
        return jnp.stack([bit[b], 1.0 - bit[b]]).reshape(2, 1, 1)

    masks = [4 * (r >> 1) + (r & 1) for r in range(4)]
    handled = place % 8
    order_heads = jnp.stack([(handled ^ m) * per for m in masks] + [(handled ^ m ^ 2) * per for m in masks])

    chunks = [(0, per // 2), (per // 2, per // 2)]
    done = None
    work = []
    for first, count in chunks:
        width = count * HEAD_DIM
        order = ((order_heads + first) // count).astype(jnp.int32)
        with jax.named_scope("states"):
            mine, sent, most = states(order, arrays, width)
        with jax.named_scope("core_exchange"):
            peer = move(sent, 2)
            peer_most = move(most, 2)
            exps = exponents(jnp.maximum(most, peer_most))
        with jax.named_scope("up"):
            got = [None] * 4
            for r in (1, 2, 3):
                got[r] = move(encode([mine[r], peer[r]], exps), masks[r])
            blocks = {(0, 0): mine[0], (1, 0): peer[0]}
            bound = 2.0 * jnp.exp2(exps)
            for r in (1, 2, 3):
                e = exponents_of(got[r])
                bound = bound + 2.0 * jnp.exp2(e)
                halves = got[r][:-TAIL].reshape(2, 2, width, HEAD_DIM)
                for c in (0, 1):
                    blocks[c, r] = decode(halves[c], e, 2)
            total = functools.reduce(jnp.add, blocks.values())
        with jax.named_scope("outer"):
            entering = jnp.zeros_like(total)
            running, running_bound = total, bound
            entering_bound = jnp.zeros_like(bound)
            for b in range(outer):
                mask = ((2 << b) - 1) << 3
                w = weight(3 + b)
                w_rows = jnp.repeat(w.reshape(2, 1), 8, axis=0)
                e = exponents(running_bound)
                if b < outer - 1:
                    reply = move(encode([running], e), mask)
                    e = exponents_of(reply)
                    other = decode(reply[:-TAIL], e, 2)
                    entering = entering + w * other
                    running = running + other
                    running_bound = running_bound + jnp.exp2(e)
                else:
                    up = bit[3 + b] > 0.5
                    payload = jnp.where(up, running[1], running[0])
                    e = jnp.tile(jnp.where(up, e[8:], e[:8]), (2, 1))
                    reply = move(encode([payload[None]], e), mask)
                    e = exponents_of(reply)
                    other = decode(reply[:-TAIL], e, 1)
                    entering = entering + w * other
                entering_bound = entering_bound + jnp.exp2(e)
        with jax.named_scope("down"):
            before = {}
            level = blocks
            wy, wc, wx = weight(0), weight(1), weight(2)
            pair = {(c, x): blocks[c, 2 * x] + blocks[c, 2 * x + 1] for c in (0, 1) for x in (0, 1)}
            quad = {x: pair[0, x] + pair[1, x] for x in (0, 1)}
            for c in (0, 1):
                for x in (0, 1):
                    for y in (0, 1):
                        near = blocks[c, 2 * x + 1 - y] * (wy if y == 0 else 1.0 - wy)
                        mid = pair[1 - c, x] * (wc if c == 0 else 1.0 - wc)
                        far = quad[1 - x] * (wx if x == 0 else 1.0 - wx)
                        before[c, 2 * x + y] = entering + near + mid + far
            e = exponents(entering_bound + bound)
            back = [None] * 4
            for r in (1, 2, 3):
                back[r] = move(encode([before[0, r], before[1, r]], e), masks[r])
            own_exps = e
        with jax.named_scope("core_return"):
            each = 2 * width
            parts = [encode([before[1, 0]], own_exps)]
            for r in (1, 2, 3):
                parts += [back[r][each : 2 * each], back[r][-TAIL:]]
            forward = move(jnp.concatenate(parts, axis=0), 2)
        with jax.named_scope("gradients"):
            near = [before[0, 0]]
            for r in (1, 2, 3):
                near.append(decode(back[r][:each], exponents_of(back[r]), 2))
            done = gradients(order[:4], arrays, jnp.stack(near), scale, width, done)
            pieces = forward.reshape(4, each + TAIL, HEAD_DIM)
            far = [decode(pieces[r, :each], exponents_of(pieces[r]), 2) for r in range(4)]
            done = gradients(order[4:], arrays, jnp.stack(far), scale, width, done)
    return tuple(done)


def entering(part, axis, reverse):
    count = lax.axis_size(axis)
    place = lax.axis_index(axis)
    ahead = count - 1 - place if reverse else place
    gathered = lax.all_gather(part, axis)

    def one(turn, state):
        source = count - 1 - turn if reverse else turn
        return state + lax.dynamic_index_in_dim(gathered, source, 0, False)

    return lax.fori_loop(0, ahead, one, jnp.zeros_like(part))


def split_groups(queries, key_rows, value_rows, grad_out):
    q_all, k_all, v_all, d_all = (
        lax.all_to_all(a, "head", split_axis=1, concat_axis=0, tiled=True)
        for a in (queries, key_rows, value_rows, grad_out)
    )
    rows_here = q_all.shape[0]
    heads_here = q_all.shape[1] // HEAD_DIM
    scale = (HEAD_DIM * rows_here * lax.axis_size("ctx")) ** (-0.5)
    highest = lax.Precision.HIGHEST
    block = GROUP
    nblocks = rows_here // block
    shape_four = (nblocks, block, heads_here, HEAD_DIM)
    q_four = q_all.reshape(shape_four)
    k_four = k_all.reshape(shape_four)
    v_four = v_all.reshape(shape_four)
    d_four = d_all.reshape(shape_four)
    kv_blocks = jnp.einsum("ntha,nthb->nhab", v_four, k_four, preferred_element_type=F32)
    g_blocks = jnp.einsum("ntha,nthb->nhab", d_four, q_four, preferred_element_type=F32)
    kv_before = entering(jnp.sum(kv_blocks, axis=0), "ctx", False)
    g_after = entering(jnp.sum(g_blocks, axis=0), "ctx", True)
    row_ids = lax.broadcasted_iota(jnp.int32, (nblocks, nblocks), 0)
    col_ids = lax.broadcasted_iota(jnp.int32, (nblocks, nblocks), 1)
    strict_lower = (col_ids < row_ids).astype(F32)
    strict_upper = (col_ids > row_ids).astype(F32)
    kv_in = kv_before[None] + jnp.einsum("mn,nhab->mhab", strict_lower, kv_blocks, precision=highest)
    g_in = g_after[None] + jnp.einsum("mn,nhab->mhab", strict_upper, g_blocks, precision=highest)
    later = lax.broadcasted_iota(jnp.int32, (block, block), 0)
    earlier = lax.broadcasted_iota(jnp.int32, (block, block), 1)
    causal = (later >= earlier).astype(F32)
    scores = (
        jnp.einsum("nthd,nshd->nhts", q_four, k_four, preferred_element_type=F32) * (scale * causal)
    ).astype(BF16)
    dscores = (jnp.einsum("nthd,nshd->nhts", d_four, v_four, preferred_element_type=F32) * causal).astype(BF16)
    k_float, v_float, d_float = (a.astype(F32) for a in (k_four, v_four, d_four))
    grad_q = scale * (
        jnp.einsum("nhts,nshd->nthd", dscores, k_four, preferred_element_type=F32)
        + jnp.einsum("ntha,nhab->nthb", d_float, kv_in, precision=highest)
    )
    grad_k = scale * (
        jnp.einsum("nhts,nthd->nshd", dscores, q_four, preferred_element_type=F32)
        + jnp.einsum("ntha,nhab->nthb", v_float, g_in, precision=highest)
    )
    grad_v = jnp.einsum(
        "nhts,nthd->nshd", scores, d_four, preferred_element_type=F32
    ) + scale * jnp.einsum("nthb,nhab->ntha", k_float, g_in, precision=highest)
    flat_shape = (rows_here, heads_here * HEAD_DIM)
    return tuple(
        lax.all_to_all(
            a.reshape(flat_shape).astype(BF16), "head", split_axis=0, concat_axis=1, tiled=True
        )
        for a in (grad_q, grad_k, grad_v)
    )


def per_device(*arrays):
    rows, columns = arrays[0].shape
    devices = lax.axis_size("ctx") * lax.axis_size("head")
    whole = rows == GROUP and lax.axis_size("head") == 2 and devices >= 16 and devices & (devices - 1) == 0
    if whole and columns % (16 * HEAD_DIM) == 0:
        return whole_groups(*arrays)
    return split_groups(*arrays)


def solution(mesh):
    placed = P(AXES, None)
    return jax.shard_map(
        per_device, mesh=mesh, in_specs=(placed,) * 4, out_specs=(placed,) * 3, check_vma=False
    )
```

```python
import functools

import jax
import jax.numpy as jnp
from jax import lax
from jax.experimental import pallas as pl
from jax.experimental.pallas import tpu as pltpu
from jax.sharding import PartitionSpec as P

HEAD_DIM = 128
GROUP = 128
AXES = ("ctx", "head")
F32 = jnp.float32
BF16 = jnp.bfloat16
HALF = jnp.float16
TAIL = 16
CUTS = (2, 2)
TOP = 15.0


VMEM = pl.BlockSpec(memory_space=pltpu.VMEM)
ANY = pl.BlockSpec(memory_space=pl.ANY)
NN, NT, TN = ((1,), (0,)), ((1,), (1,)), ((0,), (0,))
PLANE = (0, 1, 4, 5)
CORE = 2
CUBE = PLANE + tuple(m ^ CORE for m in PLANE)


def dot(a, b, dims):
    return lax.dot_general(a, b, (dims, ((), ())), preferred_element_type=F32)


def my_place():
    return lax.axis_index("ctx") * lax.axis_size("head") + lax.axis_index("head")


def block_columns(mask, chunk):
    first, count = chunk
    return pl.multiple_of((8 * first + ((my_place() & 7) ^ mask) * count) * HEAD_DIM, HEAD_DIM)


def state_kernel(chunks, q, k, v, d, *rest):
    outs, (held, in_sems, out_sems) = rest[: 2 * len(chunks)], rest[-3:]
    found = rest[2 * len(chunks) : -3]
    copies, leaving = {}, []
    for c, (first, count) in enumerate(chunks):
        cols = pl.ds(8 * first * HEAD_DIM, 8 * count * HEAD_DIM)
        for i, ref in ((1, k), (2, v), (3, d), (0, q)):
            copies[c, i] = pltpu.make_async_copy(ref.at[:, cols], held.at[i, :, cols], in_sems.at[c, i])
            copies[c, i].start()

    def leave(c, slot, begin, size, sem):
        rows = pl.ds(begin, size)
        copy = pltpu.make_async_copy(found[c].at[slot, rows], outs[2 * c + slot].at[rows], out_sems.at[c, sem])
        copy.start()
        leaving.append(copy)

    for c, (first, count) in enumerate(chunks):
        width = count * HEAD_DIM
        peaks = [jnp.zeros((8, HEAD_DIM), F32)] * 2
        for kind, (left, right) in enumerate(((2, 1), (3, 0))):
            copies[c, left].wait()
            copies[c, right].wait()
            for b in (4, 5, 6, 7, 0, 1, 2, 3):
                begin = block_columns(CUBE[b], chunks[c])
                for head in range(count):
                    cols = pl.ds(pl.multiple_of(begin + head * HEAD_DIM, HEAD_DIM), HEAD_DIM)
                    state = dot(held[left, :, cols], held[right, :, cols], TN)
                    start = (b % 4 * 2 + kind) * width + head * HEAD_DIM
                    found[c][b // 4, start : start + HEAD_DIM, :] = state
                    peak = jnp.max(jnp.abs(state).reshape(HEAD_DIM // 8, 8, HEAD_DIM), axis=0)
                    peaks[kind] = jnp.maximum(peaks[kind], peak)
                if kind == 1:
                    leave(c, b // 4, b % 4 * 2 * width, 2 * width, b)
        for kind in range(2):
            exps = exponents(jnp.full((8, HEAD_DIM), jnp.max(peaks[kind]), F32))
            for slot in range(2):
                row = 8 * width + kind * 8
                found[c][slot, row : row + 8, :] = exps
                found[c][slot, row + TAIL : row + TAIL + 8, :] = jnp.exp2(TOP - exps)
        for slot in range(2):
            leave(c, slot, 8 * width, 2 * TAIL, 8 + slot)
    for copy in leaving:
        copy.wait()


def states(arrays, chunks):
    rows, columns = arrays[0].shape
    flats = [jax.ShapeDtypeStruct((8 * n * HEAD_DIM + 2 * TAIL, HEAD_DIM), F32) for _, n in chunks]
    return pl.pallas_call(
        functools.partial(state_kernel, chunks),
        in_specs=[ANY] * 4,
        out_specs=(ANY,) * (2 * len(chunks)),
        out_shape=tuple(flat for flat in flats for _ in range(2)),
        scratch_shapes=[pltpu.VMEM((2,) + flat.shape, F32) for flat in flats]
        + [
            pltpu.VMEM((4, rows, columns), BF16),
            pltpu.SemaphoreType.DMA((len(chunks), 4)),
            pltpu.SemaphoreType.DMA((len(chunks), 10)),
        ],
        compiler_params=pltpu.CompilerParams(vmem_limit_bytes=56 << 20),
        cost_estimate=pl.CostEstimate(
            flops=4 * rows * columns * HEAD_DIM, bytes_accessed=24 * rows * columns, transcendentals=0
        ),
        name="group_states",
    )(*arrays)


def join_kernel(near, away, own, bound, *rest):
    messages, both, sems = rest[:3], rest[3], rest[4]
    width = (near.shape[0] - 2 * TAIL) // 8
    copies = []
    for i, ref in enumerate((near, away)):
        pieces = []
        for r in range(4):
            rows = pl.ds(2 * width * r, 2 * width + (2 * TAIL if r == 3 else 0))
            pieces.append(pltpu.make_async_copy(ref.at[rows], both.at[i, rows], sems.at[i, r]))
        copies.append(pieces)
    for r in (3, 0, 1, 2):
        for i in range(2):
            copies[i][r].start()
    for i in range(2):
        copies[i][3].wait()
        exps = both[i, 8 * width : 8 * width + TAIL, :]
        for message in messages:
            message[4 * width + i * TAIL : 4 * width + (i + 1) * TAIL, :] = exps
        bound[...] = jnp.exp2(exps) if i == 0 else bound[...] + jnp.exp2(exps)
    for r in range(4):
        for i in range(2):
            if r < 3:
                copies[i][r].wait()
            for kind in range(2):
                start = (r * 2 + kind) * width
                block = both[i, start : start + width, :]
                if r == 0:
                    own[i, kind] = block
                else:
                    row = 8 * width + TAIL + 8 * kind
                    to = (2 * i + kind) * width
                    messages[r - 1][to : to + width, :] = block * both[i, row : row + 1, :]


def join(mine, peer):
    width = (mine.shape[0] - 2 * TAIL) // 8
    message = jax.ShapeDtypeStruct((4 * width + 2 * TAIL, HEAD_DIM), F32)
    return pl.pallas_call(
        join_kernel,
        in_specs=[ANY, ANY],
        out_specs=(VMEM,) * 5,
        out_shape=(
            jax.ShapeDtypeStruct((2, 2, width, HEAD_DIM), F32),
            jax.ShapeDtypeStruct((TAIL, HEAD_DIM), F32),
            message,
            message,
            message,
        ),
        scratch_shapes=[pltpu.VMEM((2,) + mine.shape, F32), pltpu.SemaphoreType.DMA((2, 4))],
        compiler_params=pltpu.CompilerParams(vmem_limit_bytes=16 << 20),
        cost_estimate=pl.CostEstimate(
            flops=8 * width * HEAD_DIM, bytes_accessed=128 * width * HEAD_DIM, transcendentals=0
        ),
        name="join_groups",
    )(mine, peer)


def inside_kernel(scale, part, chunk, q, k, v, d, inner):
    rows, columns = q.shape
    first = lax.broadcasted_iota(jnp.int32, (rows, rows), 0)
    second = lax.broadcasted_iota(jnp.int32, (rows, rows), 1)
    for b, mask in enumerate(CUBE[4 * part : 4 * part + 4]):
        begin = block_columns(mask, chunk)
        for head in range(chunk[1]):
            cols = slice(head * HEAD_DIM, (head + 1) * HEAD_DIM)
            from_cols = pl.ds(pl.multiple_of(begin + head * HEAD_DIM, HEAD_DIM), HEAD_DIM)
            qh, kh, vh, dh = (ref[:, from_cols] for ref in (q, k, v, d))
            scores_t = jnp.where(second >= first, dot(kh, qh, NT) * scale, 0.0).astype(BF16)
            dscores_t = jnp.where(second >= first, dot(vh, dh, NT), 0.0).astype(BF16)
            dscores = jnp.where(first >= second, dot(dh, vh, NT), 0.0).astype(BF16)
            inner[b, 0, :, cols] = dot(dscores, kh, NN) * scale
            inner[b, 1, :, cols] = dot(dscores_t, qh, NN) * scale
            inner[b, 2, :, cols] = dot(scores_t, dh, NN)


def inside(arrays, part, chunk, scale):
    rows, width = arrays[0].shape[0], chunk[1] * HEAD_DIM
    return pl.pallas_call(
        functools.partial(inside_kernel, scale, part, chunk),
        in_specs=[VMEM] * 4,
        out_specs=VMEM,
        out_shape=jax.ShapeDtypeStruct((4, 3, rows, width), F32),
        compiler_params=pltpu.CompilerParams(vmem_limit_bytes=16 << 20),
        cost_estimate=pl.CostEstimate(
            flops=48 * rows * width * HEAD_DIM, bytes_accessed=80 * rows * width, transcendentals=0
        ),
        name="inside_group",
    )(*arrays)


def gradient_kernel(scale, part, picked, chunk, k, v, d, inner, *rest):
    inputs, outs, (done, sems) = rest[: len(picked)], rest[-5:-2], rest[-2:]
    first, count = chunk
    width = count * HEAD_DIM
    copies = []
    for state, b in zip(inputs, picked):
        mask = CUBE[4 * part + b]
        start = block_columns(mask, chunk)
        for head in range(count):
            cols = slice(head * HEAD_DIM, (head + 1) * HEAD_DIM)
            from_cols = pl.ds(pl.multiple_of(start + head * HEAD_DIM, HEAD_DIM), HEAD_DIM)
            kh, vh, dh = (ref[:, from_cols] for ref in (k, v, d))
            kv, g = state[0, cols, :] * scale, state[1, cols, :] * scale
            kv_hi, g_hi = kv.astype(BF16), g.astype(BF16)
            kv_lo = (kv - kv_hi.astype(F32)).astype(BF16)
            g_lo = (g - g_hi.astype(F32)).astype(BF16)
            out_q = inner[b, 0, :, cols] + (dot(dh, kv_hi, NN) + dot(dh, kv_lo, NN))
            out_k = inner[b, 1, :, cols] + (dot(vh, g_hi, NN) + dot(vh, g_lo, NN))
            out_v = inner[b, 2, :, cols] + (dot(kh, g_hi, NT) + dot(kh, g_lo, NT))
            for i, value in enumerate((out_q, out_k, out_v)):
                done[b, i, :, cols] = value.astype(BF16)
        for i in range(3):
            copy = pltpu.make_async_copy(done.at[b, i], outs[i].at[:, pl.ds(start, width)], sems.at[b, i])
            copy.start()
            copies.append(copy)
    for copy in copies:
        copy.wait()


def gradients(part, chunk, arrays, inner, blocks, scale, before):
    picked = tuple(sorted(blocks))
    rows, columns = arrays[0].shape
    width = chunk[1] * HEAD_DIM
    out = jax.ShapeDtypeStruct((rows, columns), BF16)
    extra = () if before is None else tuple(before)
    return pl.pallas_call(
        functools.partial(gradient_kernel, scale, part, picked, chunk),
        in_specs=[VMEM] * (4 + len(picked)) + [ANY] * len(extra),
        out_specs=(ANY,) * 3,
        out_shape=(out,) * 3,
        input_output_aliases={4 + len(picked) + i: i for i in range(len(extra))},
        scratch_shapes=[
            pltpu.VMEM((4, 3, rows, width), BF16),
            pltpu.SemaphoreType.DMA((4, 3)),
        ],
        compiler_params=pltpu.CompilerParams(vmem_limit_bytes=16 << 20),
        cost_estimate=pl.CostEstimate(
            flops=12 * len(picked) * rows * width * HEAD_DIM,
            bytes_accessed=18 * len(picked) * rows * width,
            transcendentals=0,
        ),
        name="gradients",
    )(*arrays[1:], inner, *(blocks[b] for b in picked), *extra)


def exponents(bound):
    return jnp.clip(jnp.ceil(jnp.log2(jnp.maximum(bound, 1e-30))) + 1.0, -100.0, 60.0)


def per_kind(rows):
    return rows.reshape(2, 8, HEAD_DIM)[:, :1, :]


def encode(parts):
    flat = [(part * per_kind(factor)[: part.shape[0]]).reshape(-1, HEAD_DIM) for part, _, factor in parts]
    return jnp.concatenate(flat + [exps for _, exps, _ in parts], axis=0).astype(HALF)


def tail(message, i, parts):
    start = message.shape[0] - (parts - i) * TAIL
    return message[start : start + TAIL].astype(F32)


def decode(rows, exps, kinds):
    factor = per_kind(jnp.exp2(exps - TOP))
    return rows.reshape(kinds, -1, HEAD_DIM).astype(F32) * factor[:kinds]


def after(values, *earlier):
    return lax.optimization_barrier((values, earlier))[0]


def whole_groups(queries, key_rows, value_rows, grad_out):
    arrays = (queries, key_rows, value_rows, grad_out)
    rows = queries.shape[0]
    heads = queries.shape[1] // HEAD_DIM
    devices = lax.axis_size("ctx") * lax.axis_size("head")
    place = my_place()
    scale = (HEAD_DIM * rows * devices) ** (-0.5)
    outer = (devices // 8).bit_length() - 1
    per = heads // 8

    def move(x, mask):
        return lax.ppermute(x, AXES, [(p, p ^ mask) for p in range(devices)])

    bit = [((place >> b) & 1).astype(F32) for b in range(3 + outer)]

    def weight(b):
        return jnp.stack([bit[b], 1.0 - bit[b]]).reshape(2, 1, 1)

    cuts = CUTS if sum(CUTS) == per else (per,)
    chunks = [(sum(cuts[:i]), count) for i, count in enumerate(cuts)]
    wy, wc, wx = weight(0), weight(1), weight(2)


    with jax.named_scope("states"):
        found = [x for chunk in chunks for x in states(arrays, (chunk,))]
        peers = [move(sent, CORE) for sent in found[1::2]]

    def send_up(mine, peer):
        with jax.named_scope("up"):
            own, bound, *messages = join(mine, peer)
            messages = [m.astype(HALF) for m in messages]
            got = [move(m, PLANE[r]) for r, m in zip((1, 2, 3), messages)]
            return (own, bound, got), messages

    def within(c, part, *earlier):
        with jax.named_scope("inside"):
            return inside(after(arrays, *earlier), part, chunks[c], scale)

    def exchange(c, state):
        first, count = chunks[c]
        width = count * HEAD_DIM
        with jax.named_scope("cube_total"):
            own, bound, got = state
            blocks = {(0, 0): own[0], (1, 0): own[1]}
            for r in (1, 2, 3):
                halves = got[r - 1][: -2 * TAIL].reshape(2, 2, width, HEAD_DIM)
                for i in (0, 1):
                    e = tail(got[r - 1], i, 2)
                    bound = bound + jnp.exp2(e)
                    blocks[i, r] = decode(halves[i], e, 2)
            total = functools.reduce(jnp.add, blocks.values())
        with jax.named_scope("outer"):
            sent_z = [total]
            entering = jnp.zeros_like(total)
            entering_bound = jnp.zeros_like(bound)
            running, running_bound = total, bound
            for b in range(outer):
                mask = 8 << b
                w = weight(3 + b)
                e = exponents(running_bound)
                if b < outer - 1:
                    sent_z.append(running)
                    reply = move(encode([(running, e, jnp.exp2(TOP - e))]), mask)
                    e = tail(reply, 0, 1)
                    other = decode(reply[:-TAIL], e, 2)
                    running = running + other
                    running_bound = running_bound + jnp.exp2(e)
                else:
                    up = bit[3 + b] > 0.5
                    payload = jnp.where(up, running[1], running[0])
                    e = jnp.tile(jnp.where(up, e[8:], e[:8]), (2, 1))
                    sent_z.append(payload)
                    reply = move(encode([(payload[None], e, jnp.exp2(TOP - e))]), mask)
                    e = tail(reply, 0, 1)
                    other = decode(reply[:-TAIL], e, 1)
                entering = entering + w * other
                entering_bound = entering_bound + jnp.exp2(e)
        with jax.named_scope("cube_before"):
            pair = {(i, x): blocks[i, 2 * x] + blocks[i, 2 * x + 1] for i in (0, 1) for x in (0, 1)}
            quad = {x: pair[0, x] + pair[1, x] for x in (0, 1)}
            local = {}
            for i in (0, 1):
                for x in (0, 1):
                    for y in (0, 1):
                        near = blocks[i, 2 * x + 1 - y] * (wy if y == 0 else 1.0 - wy)
                        mid = pair[1 - i, x] * (wc if i == 0 else 1.0 - wc)
                        far = quad[1 - x] * (wx if x == 0 else 1.0 - wx)
                        local[i, 2 * x + y] = near + mid + far
            local = lax.optimization_barrier(local)
        with jax.named_scope("down"):
            e = exponents(entering_bound + bound)
            factor = jnp.exp2(TOP - e)
            messages = [
                encode([(jnp.concatenate([local[0, r] + entering, local[1, r] + entering], 1), e, factor)])
                for r in (1, 2, 3)
            ]
            back = [move(m, PLANE[r]) for r, m in zip((1, 2, 3), messages)]
            return (local[0, 0] + entering, local[1, 0] + entering, e, factor, back), sent_z, messages

    def finish(c, state, inner, done, rounds):
        width = chunks[c][1] * HEAD_DIM
        own, other, e, factor, back = state
        near, far, handed = {0: own}, {}, {0: encode([(other, e, factor)])}
        for turn, blocks in enumerate(rounds):
            with jax.named_scope("core_return"):
                parts = []
                if turn:
                    back = after(back, done[:1])
                for r in blocks:
                    if r == 0:
                        parts.append(handed[0])
                        continue
                    m = back[r - 1]
                    both = m[:-TAIL].reshape(2, 2, width, HEAD_DIM)
                    near[r] = decode(both[:, 0], m[-TAIL:].astype(F32), 2)
                    parts += [both[:, 1].reshape(-1, HEAD_DIM), m[-TAIL:]]
                forward = move(jnp.concatenate(parts, axis=0), CORE)
            with jax.named_scope("gradients"):
                done = gradients(0, chunks[c], arrays, inner[0], {r: near[r] for r in blocks}, scale, done)
                pieces = forward.reshape(len(blocks), 2 * width + TAIL, HEAD_DIM)
                far = {r: decode(p[:-TAIL], p[-TAIL:].astype(F32), 2) for r, p in zip(blocks, pieces)}
                done = gradients(1, chunks[c], arrays, inner[1], far, scale, done)
        return done

    ups, inner, downs, done = [], [], [], None
    for c in range(len(chunks)):
        up, last = send_up(found[2 * c], peers[c])
        ups.append(up)
    for c in range(len(chunks)):
        inner.append([within(c, part, last) for part in (0, 1)])
    last = inner
    for c in range(len(chunks)):
        down, sent_z, last = exchange(c, after(ups[c], last))
        downs.append(down)
    for c in range(len(chunks)):
        final = c == len(chunks) - 1
        state = downs[c] if done is None else after(downs[c], done[:1])
        done = finish(c, state, inner[c], done, ((0, 1, 2), (3,)) if final else ((0, 1, 2, 3),))
    return tuple(done)


def entering(part, axis, reverse):
    count = lax.axis_size(axis)
    place = lax.axis_index(axis)
    ahead = count - 1 - place if reverse else place
    gathered = lax.all_gather(part, axis)

    def one(turn, state):
        source = count - 1 - turn if reverse else turn
        return state + lax.dynamic_index_in_dim(gathered, source, 0, False)

    return lax.fori_loop(0, ahead, one, jnp.zeros_like(part))


def split_groups(queries, key_rows, value_rows, grad_out):
    q_all, k_all, v_all, d_all = (
        lax.all_to_all(a, "head", split_axis=1, concat_axis=0, tiled=True)
        for a in (queries, key_rows, value_rows, grad_out)
    )
    rows_here = q_all.shape[0]
    heads_here = q_all.shape[1] // HEAD_DIM
    scale = (HEAD_DIM * rows_here * lax.axis_size("ctx")) ** (-0.5)
    highest = lax.Precision.HIGHEST
    block = GROUP
    nblocks = rows_here // block
    shape_four = (nblocks, block, heads_here, HEAD_DIM)
    q_four = q_all.reshape(shape_four)
    k_four = k_all.reshape(shape_four)
    v_four = v_all.reshape(shape_four)
    d_four = d_all.reshape(shape_four)
    kv_blocks = jnp.einsum("ntha,nthb->nhab", v_four, k_four, preferred_element_type=F32)
    g_blocks = jnp.einsum("ntha,nthb->nhab", d_four, q_four, preferred_element_type=F32)
    kv_before = entering(jnp.sum(kv_blocks, axis=0), "ctx", False)
    g_after = entering(jnp.sum(g_blocks, axis=0), "ctx", True)
    row_ids = lax.broadcasted_iota(jnp.int32, (nblocks, nblocks), 0)
    col_ids = lax.broadcasted_iota(jnp.int32, (nblocks, nblocks), 1)
    strict_lower = (col_ids < row_ids).astype(F32)
    strict_upper = (col_ids > row_ids).astype(F32)
    kv_in = kv_before[None] + jnp.einsum("mn,nhab->mhab", strict_lower, kv_blocks, precision=highest)
    g_in = g_after[None] + jnp.einsum("mn,nhab->mhab", strict_upper, g_blocks, precision=highest)
    later = lax.broadcasted_iota(jnp.int32, (block, block), 0)
    earlier = lax.broadcasted_iota(jnp.int32, (block, block), 1)
    causal = (later >= earlier).astype(F32)
    scores = (
        jnp.einsum("nthd,nshd->nhts", q_four, k_four, preferred_element_type=F32) * (scale * causal)
    ).astype(BF16)
    dscores = (jnp.einsum("nthd,nshd->nhts", d_four, v_four, preferred_element_type=F32) * causal).astype(BF16)
    k_float, v_float, d_float = (a.astype(F32) for a in (k_four, v_four, d_four))
    grad_q = scale * (
        jnp.einsum("nhts,nshd->nthd", dscores, k_four, preferred_element_type=F32)
        + jnp.einsum("ntha,nhab->nthb", d_float, kv_in, precision=highest)
    )
    grad_k = scale * (
        jnp.einsum("nhts,nthd->nshd", dscores, q_four, preferred_element_type=F32)
        + jnp.einsum("ntha,nhab->nthb", v_float, g_in, precision=highest)
    )
    grad_v = jnp.einsum(
        "nhts,nthd->nshd", scores, d_four, preferred_element_type=F32
    ) + scale * jnp.einsum("nthb,nhab->ntha", k_float, g_in, precision=highest)
    flat_shape = (rows_here, heads_here * HEAD_DIM)
    return tuple(
        lax.all_to_all(
            a.reshape(flat_shape).astype(BF16), "head", split_axis=0, concat_axis=1, tiled=True
        )
        for a in (grad_q, grad_k, grad_v)
    )


def per_device(*arrays):
    rows, columns = arrays[0].shape
    devices = lax.axis_size("ctx") * lax.axis_size("head")
    whole = rows == GROUP and lax.axis_size("head") == 2 and devices >= 16 and devices & (devices - 1) == 0
    if whole and columns % (16 * HEAD_DIM) == 0:
        return whole_groups(*arrays)
    return split_groups(*arrays)


def solution(mesh):
    placed = P(AXES, None)
    return jax.shard_map(
        per_device, mesh=mesh, in_specs=(placed,) * 4, out_specs=(placed,) * 3, check_vma=False
    )
```

```python
import functools

import jax
import jax.numpy as jnp
from jax import lax
from jax.experimental import pallas as pl
from jax.experimental.pallas import tpu as pltpu
from jax.sharding import PartitionSpec as P

HEAD_DIM = 128
GROUP = 128
AXES = ("ctx", "head")
F32 = jnp.float32
BF16 = jnp.bfloat16
HALF = jnp.float16
TAIL = 16
CUTS = (2, 2)
TOP = 15.0


VMEM = pl.BlockSpec(memory_space=pltpu.VMEM)
ANY = pl.BlockSpec(memory_space=pl.ANY)
NN, NT, TN = ((1,), (0,)), ((1,), (1,)), ((0,), (0,))
PLANE = (0, 1, 4, 5)
CORE = 2
CUBE = PLANE + tuple(m ^ CORE for m in PLANE)


def dot(a, b, dims):
    return lax.dot_general(a, b, (dims, ((), ())), preferred_element_type=F32)


def my_place():
    return lax.axis_index("ctx") * lax.axis_size("head") + lax.axis_index("head")


def block_columns(mask, chunk):
    first, count = chunk
    return pl.multiple_of((8 * first + ((my_place() & 7) ^ mask) * count) * HEAD_DIM, HEAD_DIM)


def state_kernel(chunks, q, k, v, d, *rest):
    outs, (held, in_sems, out_sems) = rest[: 2 * len(chunks)], rest[-3:]
    found = rest[2 * len(chunks) : -3]
    copies, leaving = {}, []
    for c, (first, count) in enumerate(chunks):
        cols = pl.ds(8 * first * HEAD_DIM, 8 * count * HEAD_DIM)
        for i, ref in ((1, k), (2, v), (3, d), (0, q)):
            copies[c, i] = pltpu.make_async_copy(ref.at[:, cols], held.at[i, :, cols], in_sems.at[c, i])
            copies[c, i].start()

    def leave(c, slot, begin, size, sem):
        rows = pl.ds(begin, size)
        copy = pltpu.make_async_copy(found[c].at[slot, rows], outs[2 * c + slot].at[rows], out_sems.at[c, sem])
        copy.start()
        leaving.append(copy)

    for c, (first, count) in enumerate(chunks):
        width = count * HEAD_DIM
        peaks = [jnp.zeros((8, HEAD_DIM), F32)] * 2
        for kind, (left, right) in enumerate(((2, 1), (3, 0))):
            copies[c, left].wait()
            copies[c, right].wait()
            for b in (4, 5, 6, 7, 0, 1, 2, 3):
                begin = block_columns(CUBE[b], chunks[c])
                for head in range(count):
                    cols = pl.ds(pl.multiple_of(begin + head * HEAD_DIM, HEAD_DIM), HEAD_DIM)
                    state = dot(held[left, :, cols], held[right, :, cols], TN)
                    start = (b % 4 * 2 + kind) * width + head * HEAD_DIM
                    found[c][b // 4, start : start + HEAD_DIM, :] = state
                    peak = jnp.max(jnp.abs(state).reshape(HEAD_DIM // 8, 8, HEAD_DIM), axis=0)
                    peaks[kind] = jnp.maximum(peaks[kind], peak)
                if kind == 1:
                    leave(c, b // 4, b % 4 * 2 * width, 2 * width, b)
        for kind in range(2):
            exps = exponents(jnp.full((8, HEAD_DIM), jnp.max(peaks[kind]), F32))
            for slot in range(2):
                row = 8 * width + kind * 8
                found[c][slot, row : row + 8, :] = exps
                found[c][slot, row + TAIL : row + TAIL + 8, :] = jnp.exp2(TOP - exps)
        for slot in range(2):
            leave(c, slot, 8 * width, 2 * TAIL, 8 + slot)
    for copy in leaving:
        copy.wait()


def states(arrays, chunks):
    rows, columns = arrays[0].shape
    flats = [jax.ShapeDtypeStruct((8 * n * HEAD_DIM + 2 * TAIL, HEAD_DIM), F32) for _, n in chunks]
    return pl.pallas_call(
        functools.partial(state_kernel, chunks),
        in_specs=[ANY] * 4,
        out_specs=(ANY,) * (2 * len(chunks)),
        out_shape=tuple(flat for flat in flats for _ in range(2)),
        scratch_shapes=[pltpu.VMEM((2,) + flat.shape, F32) for flat in flats]
        + [
            pltpu.VMEM((4, rows, columns), BF16),
            pltpu.SemaphoreType.DMA((len(chunks), 4)),
            pltpu.SemaphoreType.DMA((len(chunks), 10)),
        ],
        compiler_params=pltpu.CompilerParams(vmem_limit_bytes=56 << 20),
        cost_estimate=pl.CostEstimate(
            flops=4 * rows * columns * HEAD_DIM, bytes_accessed=24 * rows * columns, transcendentals=0
        ),
        name="group_states",
    )(*arrays)


def join_kernel(near, away, own, bound, *rest):
    messages, both, sems = rest[:3], rest[3], rest[4]
    width = (near.shape[0] - 2 * TAIL) // 8
    copies = []
    for i, ref in enumerate((near, away)):
        pieces = []
        for r in range(4):
            rows = pl.ds(2 * width * r, 2 * width + (2 * TAIL if r == 3 else 0))
            pieces.append(pltpu.make_async_copy(ref.at[rows], both.at[i, rows], sems.at[i, r]))
        copies.append(pieces)
    for r in (3, 0, 1, 2):
        for i in range(2):
            copies[i][r].start()
    for i in range(2):
        copies[i][3].wait()
        exps = both[i, 8 * width : 8 * width + TAIL, :]
        for message in messages:
            message[4 * width + i * TAIL : 4 * width + (i + 1) * TAIL, :] = exps
        bound[...] = jnp.exp2(exps) if i == 0 else bound[...] + jnp.exp2(exps)
    for r in range(4):
        for i in range(2):
            if r < 3:
                copies[i][r].wait()
            for kind in range(2):
                start = (r * 2 + kind) * width
                block = both[i, start : start + width, :]
                if r == 0:
                    own[i, kind] = block
                else:
                    row = 8 * width + TAIL + 8 * kind
                    to = (2 * i + kind) * width
                    messages[r - 1][to : to + width, :] = block * both[i, row : row + 1, :]


def join(mine, peer):
    width = (mine.shape[0] - 2 * TAIL) // 8
    message = jax.ShapeDtypeStruct((4 * width + 2 * TAIL, HEAD_DIM), F32)
    return pl.pallas_call(
        join_kernel,
        in_specs=[ANY, ANY],
        out_specs=(VMEM,) * 5,
        out_shape=(
            jax.ShapeDtypeStruct((2, 2, width, HEAD_DIM), F32),
            jax.ShapeDtypeStruct((TAIL, HEAD_DIM), F32),
            message,
            message,
            message,
        ),
        scratch_shapes=[pltpu.VMEM((2,) + mine.shape, F32), pltpu.SemaphoreType.DMA((2, 4))],
        compiler_params=pltpu.CompilerParams(vmem_limit_bytes=16 << 20),
        cost_estimate=pl.CostEstimate(
            flops=8 * width * HEAD_DIM, bytes_accessed=128 * width * HEAD_DIM, transcendentals=0
        ),
        name="join_groups",
    )(mine, peer)


def inside_kernel(scale, part, chunk, q, k, v, d, inner):
    rows, columns = q.shape
    first = lax.broadcasted_iota(jnp.int32, (rows, rows), 0)
    second = lax.broadcasted_iota(jnp.int32, (rows, rows), 1)
    for b, mask in enumerate(CUBE[4 * part : 4 * part + 4]):
        begin = block_columns(mask, chunk)
        for head in range(chunk[1]):
            cols = slice(head * HEAD_DIM, (head + 1) * HEAD_DIM)
            from_cols = pl.ds(pl.multiple_of(begin + head * HEAD_DIM, HEAD_DIM), HEAD_DIM)
            qh, kh, vh, dh = (ref[:, from_cols] for ref in (q, k, v, d))
            scores_t = jnp.where(second >= first, dot(kh, qh, NT) * scale, 0.0).astype(BF16)
            dscores_t = jnp.where(second >= first, dot(vh, dh, NT), 0.0).astype(BF16)
            dscores = jnp.where(first >= second, dot(dh, vh, NT), 0.0).astype(BF16)
            inner[b, 0, :, cols] = dot(dscores, kh, NN) * scale
            inner[b, 1, :, cols] = dot(dscores_t, qh, NN) * scale
            inner[b, 2, :, cols] = dot(scores_t, dh, NN)


def inside(arrays, part, chunk, scale):
    rows, width = arrays[0].shape[0], chunk[1] * HEAD_DIM
    return pl.pallas_call(
        functools.partial(inside_kernel, scale, part, chunk),
        in_specs=[VMEM] * 4,
        out_specs=VMEM,
        out_shape=jax.ShapeDtypeStruct((4, 3, rows, width), F32),
        compiler_params=pltpu.CompilerParams(vmem_limit_bytes=16 << 20),
        cost_estimate=pl.CostEstimate(
            flops=48 * rows * width * HEAD_DIM, bytes_accessed=80 * rows * width, transcendentals=0
        ),
        name="inside_group",
    )(*arrays)


def gradient_kernel(scale, part, picked, chunk, k, v, d, inner, *rest):
    inputs, outs, (done, sems) = rest[: len(picked)], rest[-5:-2], rest[-2:]
    first, count = chunk
    width = count * HEAD_DIM
    copies = []
    for state, b in zip(inputs, picked):
        mask = CUBE[4 * part + b]
        start = block_columns(mask, chunk)
        for head in range(count):
            cols = slice(head * HEAD_DIM, (head + 1) * HEAD_DIM)
            from_cols = pl.ds(pl.multiple_of(start + head * HEAD_DIM, HEAD_DIM), HEAD_DIM)
            kh, vh, dh = (ref[:, from_cols] for ref in (k, v, d))
            kv, g = state[0, cols, :] * scale, state[1, cols, :] * scale
            kv_hi, g_hi = kv.astype(BF16), g.astype(BF16)
            kv_lo = (kv - kv_hi.astype(F32)).astype(BF16)
            g_lo = (g - g_hi.astype(F32)).astype(BF16)
            out_q = inner[b, 0, :, cols] + (dot(dh, kv_hi, NN) + dot(dh, kv_lo, NN))
            out_k = inner[b, 1, :, cols] + (dot(vh, g_hi, NN) + dot(vh, g_lo, NN))
            out_v = inner[b, 2, :, cols] + (dot(kh, g_hi, NT) + dot(kh, g_lo, NT))
            for i, value in enumerate((out_q, out_k, out_v)):
                done[b, i, :, cols] = value.astype(BF16)
        for i in range(3):
            copy = pltpu.make_async_copy(done.at[b, i], outs[i].at[:, pl.ds(start, width)], sems.at[b, i])
            copy.start()
            copies.append(copy)
    for copy in copies:
        copy.wait()


def gradients(part, chunk, arrays, inner, blocks, scale, before):
    picked = tuple(sorted(blocks))
    rows, columns = arrays[0].shape
    width = chunk[1] * HEAD_DIM
    out = jax.ShapeDtypeStruct((rows, columns), BF16)
    extra = () if before is None else tuple(before)
    return pl.pallas_call(
        functools.partial(gradient_kernel, scale, part, picked, chunk),
        in_specs=[VMEM] * (4 + len(picked)) + [ANY] * len(extra),
        out_specs=(ANY,) * 3,
        out_shape=(out,) * 3,
        input_output_aliases={4 + len(picked) + i: i for i in range(len(extra))},
        scratch_shapes=[
            pltpu.VMEM((4, 3, rows, width), BF16),
            pltpu.SemaphoreType.DMA((4, 3)),
        ],
        compiler_params=pltpu.CompilerParams(vmem_limit_bytes=16 << 20),
        cost_estimate=pl.CostEstimate(
            flops=12 * len(picked) * rows * width * HEAD_DIM,
            bytes_accessed=18 * len(picked) * rows * width,
            transcendentals=0,
        ),
        name="gradients",
    )(*arrays[1:], inner, *(blocks[b] for b in picked), *extra)


def exponents(bound):
    return jnp.clip(jnp.ceil(jnp.log2(jnp.maximum(bound, 1e-30))) + 1.0, -100.0, 60.0)


def per_kind(rows):
    return rows.reshape(2, 8, HEAD_DIM)[:, :1, :]


def encode(parts):
    flat = [(part * per_kind(factor)[: part.shape[0]]).reshape(-1, HEAD_DIM) for part, _, factor in parts]
    return jnp.concatenate(flat + [exps for _, exps, _ in parts], axis=0).astype(HALF)


def tail(message, i, parts):
    start = message.shape[0] - (parts - i) * TAIL
    return message[start : start + TAIL].astype(F32)


def decode(rows, exps, kinds):
    factor = per_kind(jnp.exp2(exps - TOP))
    return rows.reshape(kinds, -1, HEAD_DIM).astype(F32) * factor[:kinds]


def after(values, *earlier):
    return lax.optimization_barrier((values, earlier))[0]


def whole_groups(queries, key_rows, value_rows, grad_out):
    arrays = (queries, key_rows, value_rows, grad_out)
    rows = queries.shape[0]
    heads = queries.shape[1] // HEAD_DIM
    devices = lax.axis_size("ctx") * lax.axis_size("head")
    place = my_place()
    scale = (HEAD_DIM * rows * devices) ** (-0.5)
    outer = (devices // 8).bit_length() - 1
    per = heads // 8

    def move(x, mask):
        return lax.ppermute(x, AXES, [(p, p ^ mask) for p in range(devices)])

    bit = [((place >> b) & 1).astype(F32) for b in range(3 + outer)]

    def weight(b):
        return jnp.stack([bit[b], 1.0 - bit[b]]).reshape(2, 1, 1)

    cuts = CUTS if sum(CUTS) == per else (per,)
    chunks = [(sum(cuts[:i]), count) for i, count in enumerate(cuts)]
    wy, wc, wx = weight(0), weight(1), weight(2)


    with jax.named_scope("states"):
        found = [x for chunk in chunks for x in states(arrays, (chunk,))]
        peers = [move(sent, CORE) for sent in found[1::2]]

    def send_up(mine, peer):
        with jax.named_scope("up"):
            own, bound, *messages = join(mine, peer)
            messages = [m.astype(HALF) for m in messages]
            got = [move(m, PLANE[r]) for r, m in zip((1, 2, 3), messages)]
            return (own, bound, got), messages

    def within(c, part, *earlier):
        with jax.named_scope("inside"):
            return inside(after(arrays, *earlier), part, chunks[c], scale)

    def exchange(c, state):
        first, count = chunks[c]
        width = count * HEAD_DIM
        with jax.named_scope("cube_total"):
            own, bound, got = state
            blocks = {(0, 0): own[0], (1, 0): own[1]}
            for r in (1, 2, 3):
                halves = got[r - 1][: -2 * TAIL].reshape(2, 2, width, HEAD_DIM)
                for i in (0, 1):
                    e = tail(got[r - 1], i, 2)
                    bound = bound + jnp.exp2(e)
                    blocks[i, r] = decode(halves[i], e, 2)
            total = functools.reduce(jnp.add, blocks.values())
        with jax.named_scope("outer"):
            sent_z = [total]
            entering = jnp.zeros_like(total)
            entering_bound = jnp.zeros_like(bound)
            running, running_bound = total, bound
            for b in range(outer):
                mask = 8 << b
                w = weight(3 + b)
                e = exponents(running_bound)
                if b < outer - 1:
                    sent_z.append(running)
                    reply = move(encode([(running, e, jnp.exp2(TOP - e))]), mask)
                    e = tail(reply, 0, 1)
                    other = decode(reply[:-TAIL], e, 2)
                    running = running + other
                    running_bound = running_bound + jnp.exp2(e)
                else:
                    up = bit[3 + b] > 0.5
                    payload = jnp.where(up, running[1], running[0])
                    e = jnp.tile(jnp.where(up, e[8:], e[:8]), (2, 1))
                    sent_z.append(payload)
                    reply = move(encode([(payload[None], e, jnp.exp2(TOP - e))]), mask)
                    e = tail(reply, 0, 1)
                    other = decode(reply[:-TAIL], e, 1)
                entering = entering + w * other
                entering_bound = entering_bound + jnp.exp2(e)
        with jax.named_scope("cube_before"):
            pair = {(i, x): blocks[i, 2 * x] + blocks[i, 2 * x + 1] for i in (0, 1) for x in (0, 1)}
            quad = {x: pair[0, x] + pair[1, x] for x in (0, 1)}
            local = {}
            for i in (0, 1):
                for x in (0, 1):
                    for y in (0, 1):
                        near = blocks[i, 2 * x + 1 - y] * (wy if y == 0 else 1.0 - wy)
                        mid = pair[1 - i, x] * (wc if i == 0 else 1.0 - wc)
                        far = quad[1 - x] * (wx if x == 0 else 1.0 - wx)
                        local[i, 2 * x + y] = near + mid + far
            local = lax.optimization_barrier(local)
        with jax.named_scope("down"):
            e = exponents(entering_bound + bound)
            factor = jnp.exp2(TOP - e)
            messages = [
                encode([(jnp.concatenate([local[0, r] + entering, local[1, r] + entering], 1), e, factor)])
                for r in (1, 2, 3)
            ]
            back = [move(m, PLANE[r]) for r, m in zip((1, 2, 3), messages)]
            return (local[0, 0] + entering, local[1, 0] + entering, e, factor, back), sent_z, messages

    def finish(c, state, inner, done, rounds):
        width = chunks[c][1] * HEAD_DIM
        own, other, e, factor, back = state
        for blocks in rounds:
            with jax.named_scope("core_return"):
                here = {r: back[r - 1] for r in blocks if r}
                if done is not None:
                    here = after(here, done[:1])
                near, parts = {}, []
                for r in blocks:
                    if r == 0:
                        near[0] = own
                        parts.append(encode([(other, e, factor)]))
                        continue
                    both = here[r][:-TAIL].reshape(2, 2, width, HEAD_DIM)
                    near[r] = decode(both[:, 0], here[r][-TAIL:].astype(F32), 2)
                    parts += [both[:, 1].reshape(-1, HEAD_DIM), here[r][-TAIL:]]
                forward = move(jnp.concatenate(parts, axis=0), CORE)
            with jax.named_scope("gradients"):
                done = gradients(0, chunks[c], arrays, inner[0], near, scale, done)
                pieces = forward.reshape(len(blocks), 2 * width + TAIL, HEAD_DIM)
                far = {r: decode(p[:-TAIL], p[-TAIL:].astype(F32), 2) for r, p in zip(blocks, pieces)}
                done = gradients(1, chunks[c], arrays, inner[1], far, scale, done)
        return done

    ups, inner, downs, done = [], [], [], None
    for c in range(len(chunks)):
        up, last = send_up(found[2 * c], peers[c])
        ups.append(up)
    for c in range(len(chunks)):
        inner.append([within(c, part, last) for part in (0, 1)])
    last = inner
    for c in range(len(chunks)):
        down, sent_z, last = exchange(c, after(ups[c], last))
        downs.append(down)
    for c in range(len(chunks)):
        done = finish(c, downs[c], inner[c], done, ((0, 1, 2, 3),))
    return tuple(done)


def entering(part, axis, reverse):
    count = lax.axis_size(axis)
    place = lax.axis_index(axis)
    ahead = count - 1 - place if reverse else place
    gathered = lax.all_gather(part, axis)

    def one(turn, state):
        source = count - 1 - turn if reverse else turn
        return state + lax.dynamic_index_in_dim(gathered, source, 0, False)

    return lax.fori_loop(0, ahead, one, jnp.zeros_like(part))


def split_groups(queries, key_rows, value_rows, grad_out):
    q_all, k_all, v_all, d_all = (
        lax.all_to_all(a, "head", split_axis=1, concat_axis=0, tiled=True)
        for a in (queries, key_rows, value_rows, grad_out)
    )
    rows_here = q_all.shape[0]
    heads_here = q_all.shape[1] // HEAD_DIM
    scale = (HEAD_DIM * rows_here * lax.axis_size("ctx")) ** (-0.5)
    highest = lax.Precision.HIGHEST
    block = GROUP
    nblocks = rows_here // block
    shape_four = (nblocks, block, heads_here, HEAD_DIM)
    q_four = q_all.reshape(shape_four)
    k_four = k_all.reshape(shape_four)
    v_four = v_all.reshape(shape_four)
    d_four = d_all.reshape(shape_four)
    kv_blocks = jnp.einsum("ntha,nthb->nhab", v_four, k_four, preferred_element_type=F32)
    g_blocks = jnp.einsum("ntha,nthb->nhab", d_four, q_four, preferred_element_type=F32)
    kv_before = entering(jnp.sum(kv_blocks, axis=0), "ctx", False)
    g_after = entering(jnp.sum(g_blocks, axis=0), "ctx", True)
    row_ids = lax.broadcasted_iota(jnp.int32, (nblocks, nblocks), 0)
    col_ids = lax.broadcasted_iota(jnp.int32, (nblocks, nblocks), 1)
    strict_lower = (col_ids < row_ids).astype(F32)
    strict_upper = (col_ids > row_ids).astype(F32)
    kv_in = kv_before[None] + jnp.einsum("mn,nhab->mhab", strict_lower, kv_blocks, precision=highest)
    g_in = g_after[None] + jnp.einsum("mn,nhab->mhab", strict_upper, g_blocks, precision=highest)
    later = lax.broadcasted_iota(jnp.int32, (block, block), 0)
    earlier = lax.broadcasted_iota(jnp.int32, (block, block), 1)
    causal = (later >= earlier).astype(F32)
    scores = (
        jnp.einsum("nthd,nshd->nhts", q_four, k_four, preferred_element_type=F32) * (scale * causal)
    ).astype(BF16)
    dscores = (jnp.einsum("nthd,nshd->nhts", d_four, v_four, preferred_element_type=F32) * causal).astype(BF16)
    k_float, v_float, d_float = (a.astype(F32) for a in (k_four, v_four, d_four))
    grad_q = scale * (
        jnp.einsum("nhts,nshd->nthd", dscores, k_four, preferred_element_type=F32)
        + jnp.einsum("ntha,nhab->nthb", d_float, kv_in, precision=highest)
    )
    grad_k = scale * (
        jnp.einsum("nhts,nthd->nshd", dscores, q_four, preferred_element_type=F32)
        + jnp.einsum("ntha,nhab->nthb", v_float, g_in, precision=highest)
    )
    grad_v = jnp.einsum(
        "nhts,nthd->nshd", scores, d_four, preferred_element_type=F32
    ) + scale * jnp.einsum("nthb,nhab->ntha", k_float, g_in, precision=highest)
    flat_shape = (rows_here, heads_here * HEAD_DIM)
    return tuple(
        lax.all_to_all(
            a.reshape(flat_shape).astype(BF16), "head", split_axis=0, concat_axis=1, tiled=True
        )
        for a in (grad_q, grad_k, grad_v)
    )


def per_device(*arrays):
    rows, columns = arrays[0].shape
    devices = lax.axis_size("ctx") * lax.axis_size("head")
    whole = rows == GROUP and lax.axis_size("head") == 2 and devices >= 16 and devices & (devices - 1) == 0
    if whole and columns % (16 * HEAD_DIM) == 0:
        return whole_groups(*arrays)
    return split_groups(*arrays)


def solution(mesh):
    placed = P(AXES, None)
    return jax.shard_map(
        per_device, mesh=mesh, in_specs=(placed,) * 4, out_specs=(placed,) * 3, check_vma=False
    )
```

```python
import functools

import jax
import jax.numpy as jnp
from jax import lax
from jax.experimental import pallas as pl
from jax.experimental.pallas import tpu as pltpu
from jax.sharding import PartitionSpec as P

HEAD_DIM = 128
GROUP = 128
AXES = ("ctx", "head")
F32 = jnp.float32
BF16 = jnp.bfloat16
HALF = jnp.float16
TAIL = 16
CUTS = (2, 2)
TOP = 15.0


VMEM = pl.BlockSpec(memory_space=pltpu.VMEM)
ANY = pl.BlockSpec(memory_space=pl.ANY)
NN, NT, TN = ((1,), (0,)), ((1,), (1,)), ((0,), (0,))
PLANE = (0, 1, 4, 5)
CORE = 2
CUBE = PLANE + tuple(m ^ CORE for m in PLANE)


def dot(a, b, dims):
    return lax.dot_general(a, b, (dims, ((), ())), preferred_element_type=F32)


def my_place():
    return lax.axis_index("ctx") * lax.axis_size("head") + lax.axis_index("head")


def block_columns(mask, chunk):
    first, count = chunk
    return pl.multiple_of((8 * first + ((my_place() & 7) ^ mask) * count) * HEAD_DIM, HEAD_DIM)


def state_kernel(chunk, q, k, v, d, mine, sent, held, found, in_sems, out_sems):
    first, count = chunk
    width = count * HEAD_DIM
    place = my_place()
    here = 2 * ((place >> 2) & 1) + (place & 1)
    arriving, leaving = {}, []
    for half in (1, 0):
        core = ((place >> 1) & 1) ^ half
        for i, ref in ((1, k), (2, v), (3, d), (0, q)):
            for x in range(2):
                begin = pl.multiple_of((8 * first + (4 * x + 2 * core) * count) * HEAD_DIM, HEAD_DIM)
                source = ref.at[:, pl.ds(begin, 2 * width)]
                to = held.at[half, i, :, pl.ds(2 * x * width, 2 * width)]
                arriving[half, i, x] = pltpu.make_async_copy(source, to, in_sems.at[half, i, x])
                arriving[half, i, x].start()
    for half in (1, 0):
        out = found if half else mine
        exps = []
        for kind, (left, right) in enumerate(((2, 1), (3, 0))):
            for x in range(2):
                arriving[half, left, x].wait()
                arriving[half, right, x].wait()
            peaks = jnp.zeros((8, HEAD_DIM), F32)
            for b in range(4):
                for head in range(count):
                    cols = pl.ds(pl.multiple_of(((here ^ b) * count + head) * HEAD_DIM, HEAD_DIM), HEAD_DIM)
                    state = dot(held[half, left, :, cols], held[half, right, :, cols], TN)
                    start = (kind * 4 + b) * width + head * HEAD_DIM
                    out[start : start + HEAD_DIM, :] = state
                    peak = jnp.max(jnp.abs(state).reshape(HEAD_DIM // 8, 8, HEAD_DIM), axis=0)
                    peaks = jnp.maximum(peaks, peak)
            rows = pl.ds(4 * kind * width, 4 * width)
            if half:
                leaving.append(pltpu.make_async_copy(out.at[rows], sent.at[rows], out_sems.at[kind]))
                leaving[-1].start()
            for shift in (4, 2, 1):
                peaks = jnp.maximum(peaks, pltpu.roll(peaks, shift, 0))
            exps.append(peaks)
        for kind, peaks in enumerate(exps):
            both = exponents(jnp.broadcast_to(jnp.max(peaks, axis=1, keepdims=True), peaks.shape))
            row = 8 * width + kind * 8
            out[row : row + 8, :] = both
            out[row + TAIL : row + TAIL + 8, :] = jnp.exp2(TOP - both)
        rows = pl.ds(8 * width, 2 * TAIL)
        if half:
            leaving.append(pltpu.make_async_copy(out.at[rows], sent.at[rows], out_sems.at[2]))
            leaving[-1].start()
    for copy in leaving:
        copy.wait()


def states(arrays, chunk):
    rows, columns = arrays[0].shape
    width = chunk[1] * HEAD_DIM
    flat = jax.ShapeDtypeStruct((8 * width + 2 * TAIL, HEAD_DIM), F32)
    return pl.pallas_call(
        functools.partial(state_kernel, chunk),
        in_specs=[ANY] * 4,
        out_specs=(VMEM, ANY),
        out_shape=(flat, flat),
        scratch_shapes=[
            pltpu.VMEM((2, 4, rows, 4 * width), BF16),
            pltpu.VMEM(flat.shape, F32),
            pltpu.SemaphoreType.DMA((2, 4, 2)),
            pltpu.SemaphoreType.DMA((3,)),
        ],
        compiler_params=pltpu.CompilerParams(vmem_limit_bytes=16 << 20),
        cost_estimate=pl.CostEstimate(
            flops=32 * rows * width * HEAD_DIM, bytes_accessed=128 * rows * width, transcendentals=0
        ),
        name="group_states",
    )(*arrays)


def join_kernel(near, away, own, bound, *rest):
    messages, peer, sems = rest[:3], rest[3], rest[4]
    width = (near.shape[0] - 2 * TAIL) // 8
    copies = {}
    for kind in (1, 0):
        rows = pl.ds(4 * kind * width, 4 * width + 2 * TAIL * kind)
        copies[kind] = pltpu.make_async_copy(away.at[rows], peer.at[rows], sems.at[kind])
        copies[kind].start()
    for kind in (1, 0):
        for i, ref in enumerate((near, peer)):
            if i:
                copies[kind].wait()
            if kind == 1:
                exps = ref[8 * width : 8 * width + TAIL, :]
                for message in messages:
                    message[4 * width + i * TAIL : 4 * width + (i + 1) * TAIL, :] = exps
                bound[...] = jnp.exp2(exps) if i == 0 else bound[...] + jnp.exp2(exps)
            for r in range(4):
                start = (kind * 4 + r) * width
                block = ref[start : start + width, :]
                if r == 0:
                    own[i, kind] = block
                else:
                    row = 8 * width + TAIL + 8 * kind
                    to = (2 * i + kind) * width
                    messages[r - 1][to : to + width, :] = block * ref[row : row + 1, :]


def join(mine, peer):
    width = (mine.shape[0] - 2 * TAIL) // 8
    message = jax.ShapeDtypeStruct((4 * width + 2 * TAIL, HEAD_DIM), F32)
    return pl.pallas_call(
        join_kernel,
        in_specs=[VMEM, ANY],
        out_specs=(VMEM,) * 5,
        out_shape=(
            jax.ShapeDtypeStruct((2, 2, width, HEAD_DIM), F32),
            jax.ShapeDtypeStruct((TAIL, HEAD_DIM), F32),
            message,
            message,
            message,
        ),
        scratch_shapes=[pltpu.VMEM(mine.shape, F32), pltpu.SemaphoreType.DMA((2,))],
        compiler_params=pltpu.CompilerParams(vmem_limit_bytes=16 << 20),
        cost_estimate=pl.CostEstimate(
            flops=8 * width * HEAD_DIM, bytes_accessed=128 * width * HEAD_DIM, transcendentals=0
        ),
        name="join_groups",
    )(mine, peer)


def inside_kernel(scale, part, chunk, q, k, v, d, inner):
    rows, columns = q.shape
    first = lax.broadcasted_iota(jnp.int32, (rows, rows), 0)
    second = lax.broadcasted_iota(jnp.int32, (rows, rows), 1)
    for b, mask in enumerate(CUBE[4 * part : 4 * part + 4]):
        begin = block_columns(mask, chunk)
        for head in range(chunk[1]):
            cols = slice(head * HEAD_DIM, (head + 1) * HEAD_DIM)
            from_cols = pl.ds(pl.multiple_of(begin + head * HEAD_DIM, HEAD_DIM), HEAD_DIM)
            qh, kh, vh, dh = (ref[:, from_cols] for ref in (q, k, v, d))
            scores_t = jnp.where(second >= first, dot(kh, qh, NT) * scale, 0.0).astype(BF16)
            dscores_t = jnp.where(second >= first, dot(vh, dh, NT), 0.0).astype(BF16)
            dscores = jnp.where(first >= second, dot(dh, vh, NT), 0.0).astype(BF16)
            inner[b, 0, :, cols] = dot(dscores, kh, NN) * scale
            inner[b, 1, :, cols] = dot(dscores_t, qh, NN) * scale
            inner[b, 2, :, cols] = dot(scores_t, dh, NN)


def inside(arrays, part, chunk, scale):
    rows, width = arrays[0].shape[0], chunk[1] * HEAD_DIM
    return pl.pallas_call(
        functools.partial(inside_kernel, scale, part, chunk),
        in_specs=[VMEM] * 4,
        out_specs=VMEM,
        out_shape=jax.ShapeDtypeStruct((4, 3, rows, width), F32),
        compiler_params=pltpu.CompilerParams(vmem_limit_bytes=16 << 20),
        cost_estimate=pl.CostEstimate(
            flops=48 * rows * width * HEAD_DIM, bytes_accessed=80 * rows * width, transcendentals=0
        ),
        name="inside_group",
    )(*arrays)


def gradient_kernel(scale, part, picked, chunk, k, v, d, inner, *rest):
    inputs, outs, (done, sems) = rest[: len(picked)], rest[-5:-2], rest[-2:]
    first, count = chunk
    width = count * HEAD_DIM
    copies = []
    for state, b in zip(inputs, picked):
        mask = CUBE[4 * part + b]
        start = block_columns(mask, chunk)
        for head in range(count):
            cols = slice(head * HEAD_DIM, (head + 1) * HEAD_DIM)
            from_cols = pl.ds(pl.multiple_of(start + head * HEAD_DIM, HEAD_DIM), HEAD_DIM)
            kh, vh, dh = (ref[:, from_cols] for ref in (k, v, d))
            kv, g = state[0, cols, :] * scale, state[1, cols, :] * scale
            kv_hi, g_hi = kv.astype(BF16), g.astype(BF16)
            kv_lo = (kv - kv_hi.astype(F32)).astype(BF16)
            g_lo = (g - g_hi.astype(F32)).astype(BF16)
            out_q = inner[b, 0, :, cols] + (dot(dh, kv_hi, NN) + dot(dh, kv_lo, NN))
            out_k = inner[b, 1, :, cols] + (dot(vh, g_hi, NN) + dot(vh, g_lo, NN))
            out_v = inner[b, 2, :, cols] + (dot(kh, g_hi, NT) + dot(kh, g_lo, NT))
            for i, value in enumerate((out_q, out_k, out_v)):
                done[b, i, :, cols] = value.astype(BF16)
        for i in range(3):
            copy = pltpu.make_async_copy(done.at[b, i], outs[i].at[:, pl.ds(start, width)], sems.at[b, i])
            copy.start()
            copies.append(copy)
    for copy in copies:
        copy.wait()


def gradients(part, chunk, arrays, inner, blocks, scale, before):
    picked = tuple(sorted(blocks))
    rows, columns = arrays[0].shape
    width = chunk[1] * HEAD_DIM
    out = jax.ShapeDtypeStruct((rows, columns), BF16)
    extra = () if before is None else tuple(before)
    return pl.pallas_call(
        functools.partial(gradient_kernel, scale, part, picked, chunk),
        in_specs=[VMEM] * (4 + len(picked)) + [ANY] * len(extra),
        out_specs=(ANY,) * 3,
        out_shape=(out,) * 3,
        input_output_aliases={4 + len(picked) + i: i for i in range(len(extra))},
        scratch_shapes=[
            pltpu.VMEM((4, 3, rows, width), BF16),
            pltpu.SemaphoreType.DMA((4, 3)),
        ],
        compiler_params=pltpu.CompilerParams(vmem_limit_bytes=16 << 20),
        cost_estimate=pl.CostEstimate(
            flops=12 * len(picked) * rows * width * HEAD_DIM,
            bytes_accessed=18 * len(picked) * rows * width,
            transcendentals=0,
        ),
        name="gradients",
    )(*arrays[1:], inner, *(blocks[b] for b in picked), *extra)


def exponents(bound):
    return jnp.clip(jnp.ceil(jnp.log2(jnp.maximum(bound, 1e-30))) + 1.0, -100.0, 60.0)


def per_kind(rows):
    return rows.reshape(2, 8, HEAD_DIM)[:, :1, :]


def encode(parts):
    flat = [(part * per_kind(factor)[: part.shape[0]]).reshape(-1, HEAD_DIM) for part, _, factor in parts]
    return jnp.concatenate(flat + [exps for _, exps, _ in parts], axis=0).astype(HALF)


def tail(message, i, parts):
    start = message.shape[0] - (parts - i) * TAIL
    return message[start : start + TAIL].astype(F32)


def decode(rows, exps, kinds):
    factor = per_kind(jnp.exp2(exps - TOP))
    return rows.reshape(kinds, -1, HEAD_DIM).astype(F32) * factor[:kinds]


def after(values, *earlier):
    return lax.optimization_barrier((values, earlier))[0]


def whole_groups(queries, key_rows, value_rows, grad_out):
    arrays = (queries, key_rows, value_rows, grad_out)
    rows = queries.shape[0]
    heads = queries.shape[1] // HEAD_DIM
    devices = lax.axis_size("ctx") * lax.axis_size("head")
    place = my_place()
    scale = (HEAD_DIM * rows * devices) ** (-0.5)
    outer = (devices // 8).bit_length() - 1
    per = heads // 8

    def move(x, mask):
        return lax.ppermute(x, AXES, [(p, p ^ mask) for p in range(devices)])

    bit = [((place >> b) & 1).astype(F32) for b in range(3 + outer)]

    def weight(b):
        return jnp.stack([bit[b], 1.0 - bit[b]]).reshape(2, 1, 1)

    cuts = CUTS if sum(CUTS) == per else (per,)
    chunks = [(sum(cuts[:i]), count) for i, count in enumerate(cuts)]
    wy, wc, wx = weight(0), weight(1), weight(2)


    with jax.named_scope("states"):
        placed = tuple(pltpu.with_memory_space_constraint(a, pltpu.HBM) for a in arrays)
        found = [x for chunk in chunks for x in states(placed, chunk)]
        peers = [move(sent, CORE) for sent in found[1::2]]

    def send_up(mine, peer):
        with jax.named_scope("up"):
            own, bound, *messages = join(mine, peer)
            messages = [m.astype(HALF) for m in messages]
            got = [move(m, PLANE[r]) for r, m in zip((1, 2, 3), messages)]
            return (own, bound, got), messages

    def within(c, part, *earlier):
        with jax.named_scope("inside"):
            return inside(after(arrays, *earlier), part, chunks[c], scale)

    def exchange(c, state):
        first, count = chunks[c]
        width = count * HEAD_DIM
        with jax.named_scope("cube_total"):
            own, bound, got = state
            blocks = {(0, 0): own[0], (1, 0): own[1]}
            for r in (1, 2, 3):
                halves = got[r - 1][: -2 * TAIL].reshape(2, 2, width, HEAD_DIM)
                for i in (0, 1):
                    e = tail(got[r - 1], i, 2)
                    bound = bound + jnp.exp2(e)
                    blocks[i, r] = decode(halves[i], e, 2)
            total = functools.reduce(jnp.add, blocks.values())
        with jax.named_scope("outer"):
            sent_z = [total]
            entering = jnp.zeros_like(total)
            entering_bound = jnp.zeros_like(bound)
            running, running_bound = total, bound
            for b in range(outer):
                mask = 8 << b
                w = weight(3 + b)
                e = exponents(running_bound)
                if b < outer - 1:
                    sent_z.append(running)
                    reply = move(encode([(running, e, jnp.exp2(TOP - e))]), mask)
                    e = tail(reply, 0, 1)
                    other = decode(reply[:-TAIL], e, 2)
                    running = running + other
                    running_bound = running_bound + jnp.exp2(e)
                else:
                    up = bit[3 + b] > 0.5
                    payload = jnp.where(up, running[1], running[0])
                    e = jnp.tile(jnp.where(up, e[8:], e[:8]), (2, 1))
                    sent_z.append(payload)
                    reply = move(encode([(payload[None], e, jnp.exp2(TOP - e))]), mask)
                    e = tail(reply, 0, 1)
                    other = decode(reply[:-TAIL], e, 1)
                entering = entering + w * other
                entering_bound = entering_bound + jnp.exp2(e)
        with jax.named_scope("cube_before"):
            pair = {(i, x): blocks[i, 2 * x] + blocks[i, 2 * x + 1] for i in (0, 1) for x in (0, 1)}
            quad = {x: pair[0, x] + pair[1, x] for x in (0, 1)}
            local = {}
            for i in (0, 1):
                for x in (0, 1):
                    for y in (0, 1):
                        near = blocks[i, 2 * x + 1 - y] * (wy if y == 0 else 1.0 - wy)
                        mid = pair[1 - i, x] * (wc if i == 0 else 1.0 - wc)
                        far = quad[1 - x] * (wx if x == 0 else 1.0 - wx)
                        local[i, 2 * x + y] = near + mid + far
            local = lax.optimization_barrier(local)
        with jax.named_scope("down"):
            e = exponents(entering_bound + bound)
            factor = jnp.exp2(TOP - e)
            messages = [
                encode([(jnp.concatenate([local[0, r] + entering, local[1, r] + entering], 1), e, factor)])
                for r in (1, 2, 3)
            ]
            back = [move(m, PLANE[r]) for r, m in zip((1, 2, 3), messages)]
            return (local[0, 0] + entering, local[1, 0] + entering, e, factor, back), sent_z, messages

    def finish(c, state, inner, done, rounds):
        width = chunks[c][1] * HEAD_DIM
        own, other, e, factor, back = state
        for blocks in rounds:
            with jax.named_scope("core_return"):
                here = {r: back[r - 1] for r in blocks if r}
                if done is not None:
                    here = after(here, done[:1])
                near, parts = {}, []
                for r in blocks:
                    if r == 0:
                        near[0] = own
                        parts.append(encode([(other, e, factor)]))
                        continue
                    both = here[r][:-TAIL].reshape(2, 2, width, HEAD_DIM)
                    near[r] = decode(both[:, 0], here[r][-TAIL:].astype(F32), 2)
                    parts += [both[:, 1].reshape(-1, HEAD_DIM), here[r][-TAIL:]]
                forward = move(jnp.concatenate(parts, axis=0), CORE)
            with jax.named_scope("gradients"):
                done = gradients(0, chunks[c], arrays, inner[0], near, scale, done)
                pieces = forward.reshape(len(blocks), 2 * width + TAIL, HEAD_DIM)
                far = {r: decode(p[:-TAIL], p[-TAIL:].astype(F32), 2) for r, p in zip(blocks, pieces)}
                done = gradients(1, chunks[c], arrays, inner[1], far, scale, done)
        return done

    ups, inner, downs, done = [], [], [], None
    for c in range(len(chunks)):
        up, last = send_up(found[2 * c], peers[c])
        ups.append(up)
    for c in range(len(chunks)):
        inner.append([within(c, part, last) for part in (0, 1)])
    last = inner
    for c in range(len(chunks)):
        down, sent_z, last = exchange(c, after(ups[c], last))
        downs.append(down)
    for c in range(len(chunks)):
        done = finish(c, downs[c], inner[c], done, ((0, 1, 2, 3),))
    return tuple(done)


def entering(part, axis, reverse):
    count = lax.axis_size(axis)
    place = lax.axis_index(axis)
    ahead = count - 1 - place if reverse else place
    gathered = lax.all_gather(part, axis)

    def one(turn, state):
        source = count - 1 - turn if reverse else turn
        return state + lax.dynamic_index_in_dim(gathered, source, 0, False)

    return lax.fori_loop(0, ahead, one, jnp.zeros_like(part))


def split_groups(queries, key_rows, value_rows, grad_out):
    q_all, k_all, v_all, d_all = (
        lax.all_to_all(a, "head", split_axis=1, concat_axis=0, tiled=True)
        for a in (queries, key_rows, value_rows, grad_out)
    )
    rows_here = q_all.shape[0]
    heads_here = q_all.shape[1] // HEAD_DIM
    scale = (HEAD_DIM * rows_here * lax.axis_size("ctx")) ** (-0.5)
    highest = lax.Precision.HIGHEST
    block = GROUP
    nblocks = rows_here // block
    shape_four = (nblocks, block, heads_here, HEAD_DIM)
    q_four = q_all.reshape(shape_four)
    k_four = k_all.reshape(shape_four)
    v_four = v_all.reshape(shape_four)
    d_four = d_all.reshape(shape_four)
    kv_blocks = jnp.einsum("ntha,nthb->nhab", v_four, k_four, preferred_element_type=F32)
    g_blocks = jnp.einsum("ntha,nthb->nhab", d_four, q_four, preferred_element_type=F32)
    kv_before = entering(jnp.sum(kv_blocks, axis=0), "ctx", False)
    g_after = entering(jnp.sum(g_blocks, axis=0), "ctx", True)
    row_ids = lax.broadcasted_iota(jnp.int32, (nblocks, nblocks), 0)
    col_ids = lax.broadcasted_iota(jnp.int32, (nblocks, nblocks), 1)
    strict_lower = (col_ids < row_ids).astype(F32)
    strict_upper = (col_ids > row_ids).astype(F32)
    kv_in = kv_before[None] + jnp.einsum("mn,nhab->mhab", strict_lower, kv_blocks, precision=highest)
    g_in = g_after[None] + jnp.einsum("mn,nhab->mhab", strict_upper, g_blocks, precision=highest)
    later = lax.broadcasted_iota(jnp.int32, (block, block), 0)
    earlier = lax.broadcasted_iota(jnp.int32, (block, block), 1)
    causal = (later >= earlier).astype(F32)
    scores = (
        jnp.einsum("nthd,nshd->nhts", q_four, k_four, preferred_element_type=F32) * (scale * causal)
    ).astype(BF16)
    dscores = (jnp.einsum("nthd,nshd->nhts", d_four, v_four, preferred_element_type=F32) * causal).astype(BF16)
    k_float, v_float, d_float = (a.astype(F32) for a in (k_four, v_four, d_four))
    grad_q = scale * (
        jnp.einsum("nhts,nshd->nthd", dscores, k_four, preferred_element_type=F32)
        + jnp.einsum("ntha,nhab->nthb", d_float, kv_in, precision=highest)
    )
    grad_k = scale * (
        jnp.einsum("nhts,nthd->nshd", dscores, q_four, preferred_element_type=F32)
        + jnp.einsum("ntha,nhab->nthb", v_float, g_in, precision=highest)
    )
    grad_v = jnp.einsum(
        "nhts,nthd->nshd", scores, d_four, preferred_element_type=F32
    ) + scale * jnp.einsum("nthb,nhab->ntha", k_float, g_in, precision=highest)
    flat_shape = (rows_here, heads_here * HEAD_DIM)
    return tuple(
        lax.all_to_all(
            a.reshape(flat_shape).astype(BF16), "head", split_axis=0, concat_axis=1, tiled=True
        )
        for a in (grad_q, grad_k, grad_v)
    )


def per_device(*arrays):
    rows, columns = arrays[0].shape
    devices = lax.axis_size("ctx") * lax.axis_size("head")
    whole = rows == GROUP and lax.axis_size("head") == 2 and devices >= 16 and devices & (devices - 1) == 0
    if whole and columns % (16 * HEAD_DIM) == 0:
        return whole_groups(*arrays)
    return split_groups(*arrays)


def solution(mesh):
    placed = P(AXES, None)
    return jax.shard_map(
        per_device, mesh=mesh, in_specs=(placed,) * 4, out_specs=(placed,) * 3, check_vma=False
    )
```

```python
import functools

import jax
import jax.numpy as jnp
from jax import lax
from jax.experimental import pallas as pl
from jax.experimental.pallas import tpu as pltpu
from jax.sharding import PartitionSpec as P

HEAD_DIM = 128
GROUP = 128
AXES = ("ctx", "head")
F32 = jnp.float32
BF16 = jnp.bfloat16
HALF = jnp.float16
TAIL = 16
CUTS = (2, 2)
TOP = 15.0


VMEM = pl.BlockSpec(memory_space=pltpu.VMEM)
ANY = pl.BlockSpec(memory_space=pl.ANY)
NN, NT, TN = ((1,), (0,)), ((1,), (1,)), ((0,), (0,))
PLANE = (0, 1, 4, 5)
CORE = 2
CUBE = PLANE + tuple(m ^ CORE for m in PLANE)


def dot(a, b, dims):
    return lax.dot_general(a, b, (dims, ((), ())), preferred_element_type=F32)


def my_place():
    return lax.axis_index("ctx") * lax.axis_size("head") + lax.axis_index("head")


def block_columns(mask, chunk):
    first, count = chunk
    return pl.multiple_of((8 * first + ((my_place() & 7) ^ mask) * count) * HEAD_DIM, HEAD_DIM)


def state_kernel(chunk, q, k, v, d, mine, sent, held, found, in_sems, out_sems):
    first, count = chunk
    width = count * HEAD_DIM
    place = my_place()
    here = 2 * ((place >> 2) & 1) + (place & 1)
    arriving, leaving = {}, []
    for half in (1, 0):
        core = ((place >> 1) & 1) ^ half
        for i, ref in ((1, k), (2, v), (3, d), (0, q)):
            for x in range(2):
                begin = pl.multiple_of((8 * first + (4 * x + 2 * core) * count) * HEAD_DIM, HEAD_DIM)
                source = ref.at[:, pl.ds(begin, 2 * width)]
                to = held.at[half, i, :, pl.ds(2 * x * width, 2 * width)]
                arriving[half, i, x] = pltpu.make_async_copy(source, to, in_sems.at[half, i, x])
                arriving[half, i, x].start()
    for half in (1, 0):
        out = found if half else mine
        exps = []
        for kind, (left, right) in enumerate(((2, 1), (3, 0))):
            for x in range(2):
                arriving[half, left, x].wait()
                arriving[half, right, x].wait()
            peaks = jnp.zeros((8, HEAD_DIM), F32)
            for b in range(4):
                for head in range(count):
                    cols = pl.ds(pl.multiple_of(((here ^ b) * count + head) * HEAD_DIM, HEAD_DIM), HEAD_DIM)
                    state = dot(held[half, left, :, cols], held[half, right, :, cols], TN)
                    start = (kind * 4 + b) * width + head * HEAD_DIM
                    out[start : start + HEAD_DIM, :] = state
                    peak = jnp.max(jnp.abs(state).reshape(HEAD_DIM // 8, 8, HEAD_DIM), axis=0)
                    peaks = jnp.maximum(peaks, peak)
            rows = pl.ds(4 * kind * width, 4 * width)
            if half:
                leaving.append(pltpu.make_async_copy(out.at[rows], sent.at[rows], out_sems.at[kind]))
                leaving[-1].start()
            for shift in (4, 2, 1):
                peaks = jnp.maximum(peaks, pltpu.roll(peaks, shift, 0))
            exps.append(peaks)
        for kind, peaks in enumerate(exps):
            both = exponents(jnp.broadcast_to(jnp.max(peaks, axis=1, keepdims=True), peaks.shape))
            row = 8 * width + kind * 8
            out[row : row + 8, :] = both
            out[row + TAIL : row + TAIL + 8, :] = jnp.exp2(TOP - both)
        rows = pl.ds(8 * width, 2 * TAIL)
        if half:
            leaving.append(pltpu.make_async_copy(out.at[rows], sent.at[rows], out_sems.at[2]))
            leaving[-1].start()
    for copy in leaving:
        copy.wait()


def states(arrays, chunk):
    rows, columns = arrays[0].shape
    width = chunk[1] * HEAD_DIM
    flat = jax.ShapeDtypeStruct((8 * width + 2 * TAIL, HEAD_DIM), F32)
    return pl.pallas_call(
        functools.partial(state_kernel, chunk),
        in_specs=[ANY] * 4,
        out_specs=(VMEM, ANY),
        out_shape=(flat, flat),
        scratch_shapes=[
            pltpu.VMEM((2, 4, rows, 4 * width), BF16),
            pltpu.VMEM(flat.shape, F32),
            pltpu.SemaphoreType.DMA((2, 4, 2)),
            pltpu.SemaphoreType.DMA((3,)),
        ],
        compiler_params=pltpu.CompilerParams(vmem_limit_bytes=16 << 20),
        cost_estimate=pl.CostEstimate(
            flops=32 * rows * width * HEAD_DIM, bytes_accessed=128 * rows * width, transcendentals=0
        ),
        name="group_states",
    )(*arrays)


def join_kernel(near, away, own, bound, *rest):
    messages, peer, sems = rest[:3], rest[3], rest[4]
    width = (near.shape[0] - 2 * TAIL) // 8
    copies = {}
    for kind in (1, 0):
        rows = pl.ds(4 * kind * width, 4 * width + 2 * TAIL * kind)
        copies[kind] = pltpu.make_async_copy(away.at[rows], peer.at[rows], sems.at[kind])
        copies[kind].start()
    for kind in (1, 0):
        for i, ref in enumerate((near, peer)):
            if i:
                copies[kind].wait()
            if kind == 1:
                exps = ref[8 * width : 8 * width + TAIL, :]
                for message in messages:
                    message[4 * width + i * TAIL : 4 * width + (i + 1) * TAIL, :] = exps
                bound[...] = jnp.exp2(exps) if i == 0 else bound[...] + jnp.exp2(exps)
            for r in range(4):
                start = (kind * 4 + r) * width
                block = ref[start : start + width, :]
                if r == 0:
                    own[i, kind] = block
                else:
                    row = 8 * width + TAIL + 8 * kind
                    to = (2 * i + kind) * width
                    messages[r - 1][to : to + width, :] = block * ref[row : row + 1, :]


def join(mine, peer):
    width = (mine.shape[0] - 2 * TAIL) // 8
    message = jax.ShapeDtypeStruct((4 * width + 2 * TAIL, HEAD_DIM), F32)
    return pl.pallas_call(
        join_kernel,
        in_specs=[VMEM, ANY],
        out_specs=(VMEM,) * 5,
        out_shape=(
            jax.ShapeDtypeStruct((2, 2, width, HEAD_DIM), F32),
            jax.ShapeDtypeStruct((TAIL, HEAD_DIM), F32),
            message,
            message,
            message,
        ),
        scratch_shapes=[pltpu.VMEM(mine.shape, F32), pltpu.SemaphoreType.DMA((2,))],
        compiler_params=pltpu.CompilerParams(vmem_limit_bytes=16 << 20),
        cost_estimate=pl.CostEstimate(
            flops=8 * width * HEAD_DIM, bytes_accessed=128 * width * HEAD_DIM, transcendentals=0
        ),
        name="join_groups",
    )(mine, peer)


def inside_kernel(scale, part, chunk, q, k, v, d, inner):
    rows, columns = q.shape
    first = lax.broadcasted_iota(jnp.int32, (rows, rows), 0)
    second = lax.broadcasted_iota(jnp.int32, (rows, rows), 1)
    for b, mask in enumerate(CUBE[4 * part : 4 * part + 4]):
        begin = block_columns(mask, chunk)
        for head in range(chunk[1]):
            cols = slice(head * HEAD_DIM, (head + 1) * HEAD_DIM)
            from_cols = pl.ds(pl.multiple_of(begin + head * HEAD_DIM, HEAD_DIM), HEAD_DIM)
            qh, kh, vh, dh = (ref[:, from_cols] for ref in (q, k, v, d))
            scores_t = jnp.where(second >= first, dot(kh, qh, NT) * scale, 0.0).astype(BF16)
            dscores_t = jnp.where(second >= first, dot(vh, dh, NT), 0.0).astype(BF16)
            dscores = jnp.where(first >= second, dot(dh, vh, NT), 0.0).astype(BF16)
            inner[b, 0, :, cols] = dot(dscores, kh, NN) * scale
            inner[b, 1, :, cols] = dot(dscores_t, qh, NN) * scale
            inner[b, 2, :, cols] = dot(scores_t, dh, NN)


def inside(arrays, part, chunk, scale):
    rows, width = arrays[0].shape[0], chunk[1] * HEAD_DIM
    return pl.pallas_call(
        functools.partial(inside_kernel, scale, part, chunk),
        in_specs=[VMEM] * 4,
        out_specs=VMEM,
        out_shape=jax.ShapeDtypeStruct((4, 3, rows, width), F32),
        compiler_params=pltpu.CompilerParams(vmem_limit_bytes=16 << 20),
        cost_estimate=pl.CostEstimate(
            flops=48 * rows * width * HEAD_DIM, bytes_accessed=80 * rows * width, transcendentals=0
        ),
        name="inside_group",
    )(*arrays)


def gradient_kernel(scale, part, picked, chunk, k, v, d, inner, *rest):
    inputs, outs, (done, sems) = rest[: len(picked)], rest[-5:-2], rest[-2:]
    first, count = chunk
    width = count * HEAD_DIM
    copies = []
    for state, b in zip(inputs, picked):
        mask = CUBE[4 * part + b]
        start = block_columns(mask, chunk)
        for head in range(count):
            cols = slice(head * HEAD_DIM, (head + 1) * HEAD_DIM)
            from_cols = pl.ds(pl.multiple_of(start + head * HEAD_DIM, HEAD_DIM), HEAD_DIM)
            kh, vh, dh = (ref[:, from_cols] for ref in (k, v, d))
            kv, g = state[0, cols, :] * scale, state[1, cols, :] * scale
            kv_hi, g_hi = kv.astype(BF16), g.astype(BF16)
            kv_lo = (kv - kv_hi.astype(F32)).astype(BF16)
            g_lo = (g - g_hi.astype(F32)).astype(BF16)
            out_q = inner[b, 0, :, cols] + (dot(dh, kv_hi, NN) + dot(dh, kv_lo, NN))
            out_k = inner[b, 1, :, cols] + (dot(vh, g_hi, NN) + dot(vh, g_lo, NN))
            out_v = inner[b, 2, :, cols] + (dot(kh, g_hi, NT) + dot(kh, g_lo, NT))
            for i, value in enumerate((out_q, out_k, out_v)):
                done[b, i, :, cols] = value.astype(BF16)
        for i in range(3):
            copy = pltpu.make_async_copy(done.at[b, i], outs[i].at[:, pl.ds(start, width)], sems.at[b, i])
            copy.start()
            copies.append(copy)
    for copy in copies:
        copy.wait()


def gradients(part, chunk, arrays, inner, blocks, scale, before):
    picked = tuple(sorted(blocks))
    rows, columns = arrays[0].shape
    width = chunk[1] * HEAD_DIM
    out = jax.ShapeDtypeStruct((rows, columns), BF16)
    extra = () if before is None else tuple(before)
    return pl.pallas_call(
        functools.partial(gradient_kernel, scale, part, picked, chunk),
        in_specs=[VMEM] * (4 + len(picked)) + [ANY] * len(extra),
        out_specs=(ANY,) * 3,
        out_shape=(out,) * 3,
        input_output_aliases={4 + len(picked) + i: i for i in range(len(extra))},
        scratch_shapes=[
            pltpu.VMEM((4, 3, rows, width), BF16),
            pltpu.SemaphoreType.DMA((4, 3)),
        ],
        compiler_params=pltpu.CompilerParams(vmem_limit_bytes=16 << 20),
        cost_estimate=pl.CostEstimate(
            flops=12 * len(picked) * rows * width * HEAD_DIM,
            bytes_accessed=18 * len(picked) * rows * width,
            transcendentals=0,
        ),
        name="gradients",
    )(*arrays[1:], inner, *(blocks[b] for b in picked), *extra)


def exponents(bound):
    return jnp.clip(jnp.ceil(jnp.log2(jnp.maximum(bound, 1e-30))) + 1.0, -100.0, 60.0)


def per_kind(rows):
    return rows.reshape(2, 8, HEAD_DIM)[:, :1, :]


def encode(parts):
    flat = [(part * per_kind(factor)[: part.shape[0]]).reshape(-1, HEAD_DIM) for part, _, factor in parts]
    return jnp.concatenate(flat + [exps for _, exps, _ in parts], axis=0).astype(HALF)


def tail(message, i, parts):
    start = message.shape[0] - (parts - i) * TAIL
    return message[start : start + TAIL].astype(F32)


def decode(rows, exps, kinds):
    factor = per_kind(jnp.exp2(exps - TOP))
    return rows.reshape(kinds, -1, HEAD_DIM).astype(F32) * factor[:kinds]


def after(values, *earlier):
    return lax.optimization_barrier((values, earlier))[0]


def whole_groups(queries, key_rows, value_rows, grad_out):
    arrays = (queries, key_rows, value_rows, grad_out)
    rows = queries.shape[0]
    heads = queries.shape[1] // HEAD_DIM
    devices = lax.axis_size("ctx") * lax.axis_size("head")
    place = my_place()
    scale = (HEAD_DIM * rows * devices) ** (-0.5)
    outer = (devices // 8).bit_length() - 1
    per = heads // 8

    def move(x, mask):
        return lax.ppermute(x, AXES, [(p, p ^ mask) for p in range(devices)])

    bit = [((place >> b) & 1).astype(F32) for b in range(3 + outer)]

    def weight(b):
        return jnp.stack([bit[b], 1.0 - bit[b]]).reshape(2, 1, 1)

    cuts = CUTS if sum(CUTS) == per else (per,)
    chunks = [(sum(cuts[:i]), count) for i, count in enumerate(cuts)]
    wy, wc, wx = weight(0), weight(1), weight(2)


    with jax.named_scope("states"):
        placed = tuple(pltpu.with_memory_space_constraint(a, pltpu.HBM) for a in arrays)
        found = [x for chunk in chunks for x in states(placed, chunk)]
        peers = [move(sent, CORE) for sent in found[1::2]]

    def send_up(mine, peer):
        with jax.named_scope("up"):
            own, bound, *messages = join(mine, peer)
            messages = [m.astype(HALF) for m in messages]
            got = [move(m, PLANE[r]) for r, m in zip((1, 2, 3), messages)]
            return (own, bound, got), messages

    def within(c, part, *earlier):
        with jax.named_scope("inside"):
            return inside(after(arrays, *earlier), part, chunks[c], scale)

    def exchange(c, state):
        first, count = chunks[c]
        width = count * HEAD_DIM
        with jax.named_scope("cube_total"):
            own, bound, got = state
            blocks = {(0, 0): own[0], (1, 0): own[1]}
            for r in (1, 2, 3):
                halves = got[r - 1][: -2 * TAIL].reshape(2, 2, width, HEAD_DIM)
                for i in (0, 1):
                    e = tail(got[r - 1], i, 2)
                    bound = bound + jnp.exp2(e)
                    blocks[i, r] = decode(halves[i], e, 2)
            total = functools.reduce(jnp.add, blocks.values())
        with jax.named_scope("outer"):
            sent_z = [total]
            entering = jnp.zeros_like(total)
            entering_bound = jnp.zeros_like(bound)
            running, running_bound = total, bound
            for b in range(outer):
                mask = 8 << b
                w = weight(3 + b)
                e = exponents(running_bound)
                if b < outer - 1:
                    sent_z.append(running)
                    reply = move(encode([(running, e, jnp.exp2(TOP - e))]), mask)
                    e = tail(reply, 0, 1)
                    other = decode(reply[:-TAIL], e, 2)
                    running = running + other
                    running_bound = running_bound + jnp.exp2(e)
                else:
                    up = bit[3 + b] > 0.5
                    payload = jnp.where(up, running[1], running[0])
                    e = jnp.tile(jnp.where(up, e[8:], e[:8]), (2, 1))
                    sent_z.append(payload)
                    reply = move(encode([(payload[None], e, jnp.exp2(TOP - e))]), mask)
                    e = tail(reply, 0, 1)
                    other = decode(reply[:-TAIL], e, 1)
                entering = entering + w * other
                came = jnp.repeat(w.reshape(2, 1), 8, axis=0)
                entering_bound = entering_bound + came * jnp.exp2(e)
        with jax.named_scope("cube_before"):
            pair = {(i, x): blocks[i, 2 * x] + blocks[i, 2 * x + 1] for i in (0, 1) for x in (0, 1)}
            quad = {x: pair[0, x] + pair[1, x] for x in (0, 1)}
            local = {}
            for i in (0, 1):
                for x in (0, 1):
                    for y in (0, 1):
                        near = blocks[i, 2 * x + 1 - y] * (wy if y == 0 else 1.0 - wy)
                        mid = pair[1 - i, x] * (wc if i == 0 else 1.0 - wc)
                        far = quad[1 - x] * (wx if x == 0 else 1.0 - wx)
                        local[i, 2 * x + y] = near + mid + far
            local = lax.optimization_barrier(local)
        with jax.named_scope("down"):
            e = exponents(entering_bound + bound)
            factor = jnp.exp2(TOP - e)
            messages = [
                encode([(jnp.concatenate([local[0, r] + entering, local[1, r] + entering], 1), e, factor)])
                for r in (1, 2, 3)
            ]
            back = [move(m, PLANE[r]) for r, m in zip((1, 2, 3), messages)]
            return (local[0, 0] + entering, local[1, 0] + entering, e, factor, back), sent_z, messages

    def finish(c, state, inner, done, rounds):
        width = chunks[c][1] * HEAD_DIM
        own, other, e, factor, back = state
        for blocks in rounds:
            with jax.named_scope("core_return"):
                here = {r: back[r - 1] for r in blocks if r}
                if done is not None:
                    here = after(here, done[:1])
                near, parts = {}, []
                for r in blocks:
                    if r == 0:
                        near[0] = own
                        parts.append(encode([(other, e, factor)]))
                        continue
                    both = here[r][:-TAIL].reshape(2, 2, width, HEAD_DIM)
                    near[r] = decode(both[:, 0], here[r][-TAIL:].astype(F32), 2)
                    parts += [both[:, 1].reshape(-1, HEAD_DIM), here[r][-TAIL:]]
                forward = move(jnp.concatenate(parts, axis=0), CORE)
            with jax.named_scope("gradients"):
                done = gradients(0, chunks[c], arrays, inner[0], near, scale, done)
                pieces = forward.reshape(len(blocks), 2 * width + TAIL, HEAD_DIM)
                far = {r: decode(p[:-TAIL], p[-TAIL:].astype(F32), 2) for r, p in zip(blocks, pieces)}
                done = gradients(1, chunks[c], arrays, inner[1], far, scale, done)
        return done

    ups, inner, downs, done = [], [], [], None
    for c in range(len(chunks)):
        up, last = send_up(found[2 * c], peers[c])
        ups.append(up)
    for c in range(len(chunks)):
        inner.append([within(c, part, last) for part in (0, 1)])
    last = inner
    for c in range(len(chunks)):
        down, sent_z, last = exchange(c, after(ups[c], last))
        downs.append(down)
    for c in range(len(chunks)):
        done = finish(c, downs[c], inner[c], done, ((0, 1, 2, 3),))
    return tuple(done)


def entering(part, axis, reverse):
    count = lax.axis_size(axis)
    place = lax.axis_index(axis)
    ahead = count - 1 - place if reverse else place
    gathered = lax.all_gather(part, axis)

    def one(turn, state):
        source = count - 1 - turn if reverse else turn
        return state + lax.dynamic_index_in_dim(gathered, source, 0, False)

    return lax.fori_loop(0, ahead, one, jnp.zeros_like(part))


def split_groups(queries, key_rows, value_rows, grad_out):
    q_all, k_all, v_all, d_all = (
        lax.all_to_all(a, "head", split_axis=1, concat_axis=0, tiled=True)
        for a in (queries, key_rows, value_rows, grad_out)
    )
    rows_here = q_all.shape[0]
    heads_here = q_all.shape[1] // HEAD_DIM
    scale = (HEAD_DIM * rows_here * lax.axis_size("ctx")) ** (-0.5)
    highest = lax.Precision.HIGHEST
    block = GROUP
    nblocks = rows_here // block
    shape_four = (nblocks, block, heads_here, HEAD_DIM)
    q_four = q_all.reshape(shape_four)
    k_four = k_all.reshape(shape_four)
    v_four = v_all.reshape(shape_four)
    d_four = d_all.reshape(shape_four)
    kv_blocks = jnp.einsum("ntha,nthb->nhab", v_four, k_four, preferred_element_type=F32)
    g_blocks = jnp.einsum("ntha,nthb->nhab", d_four, q_four, preferred_element_type=F32)
    kv_before = entering(jnp.sum(kv_blocks, axis=0), "ctx", False)
    g_after = entering(jnp.sum(g_blocks, axis=0), "ctx", True)
    row_ids = lax.broadcasted_iota(jnp.int32, (nblocks, nblocks), 0)
    col_ids = lax.broadcasted_iota(jnp.int32, (nblocks, nblocks), 1)
    strict_lower = (col_ids < row_ids).astype(F32)
    strict_upper = (col_ids > row_ids).astype(F32)
    kv_in = kv_before[None] + jnp.einsum("mn,nhab->mhab", strict_lower, kv_blocks, precision=highest)
    g_in = g_after[None] + jnp.einsum("mn,nhab->mhab", strict_upper, g_blocks, precision=highest)
    later = lax.broadcasted_iota(jnp.int32, (block, block), 0)
    earlier = lax.broadcasted_iota(jnp.int32, (block, block), 1)
    causal = (later >= earlier).astype(F32)
    scores = (
        jnp.einsum("nthd,nshd->nhts", q_four, k_four, preferred_element_type=F32) * (scale * causal)
    ).astype(BF16)
    dscores = (jnp.einsum("nthd,nshd->nhts", d_four, v_four, preferred_element_type=F32) * causal).astype(BF16)
    k_float, v_float, d_float = (a.astype(F32) for a in (k_four, v_four, d_four))
    grad_q = scale * (
        jnp.einsum("nhts,nshd->nthd", dscores, k_four, preferred_element_type=F32)
        + jnp.einsum("ntha,nhab->nthb", d_float, kv_in, precision=highest)
    )
    grad_k = scale * (
        jnp.einsum("nhts,nthd->nshd", dscores, q_four, preferred_element_type=F32)
        + jnp.einsum("ntha,nhab->nthb", v_float, g_in, precision=highest)
    )
    grad_v = jnp.einsum(
        "nhts,nthd->nshd", scores, d_four, preferred_element_type=F32
    ) + scale * jnp.einsum("nthb,nhab->ntha", k_float, g_in, precision=highest)
    flat_shape = (rows_here, heads_here * HEAD_DIM)
    return tuple(
        lax.all_to_all(
            a.reshape(flat_shape).astype(BF16), "head", split_axis=0, concat_axis=1, tiled=True
        )
        for a in (grad_q, grad_k, grad_v)
    )


def per_device(*arrays):
    rows, columns = arrays[0].shape
    devices = lax.axis_size("ctx") * lax.axis_size("head")
    whole = rows == GROUP and lax.axis_size("head") == 2 and devices >= 16 and devices & (devices - 1) == 0
    if whole and columns % (16 * HEAD_DIM) == 0:
        return whole_groups(*arrays)
    return split_groups(*arrays)


def solution(mesh):
    placed = P(AXES, None)
    return jax.shard_map(
        per_device, mesh=mesh, in_specs=(placed,) * 4, out_specs=(placed,) * 3, check_vma=False
    )
```
